256 devices in a mesh: dp: 16 (over x, y), tensor: 16 (over z, core).
Axes of the slice: x: 4, y: 4, z: 8, core: 2. Of those that a mesh axis runs over, the one named last changes fastest.
Arguments:
- context: bfloat16 [32, 1024, 4096], P('dp', None, 'tensor'), may hold values from -6 to 6
- out_grad: bfloat16 [32, 1024, 4608], P('dp', None, 'tensor'), may hold values from -40 to 40
- example_user: int32 [32], replicated, may hold values from 0 to 15, as said below
- user_counts: int32 [16], replicated, may hold values from 1 to 4, as said below
Outputs:
- weight_grad: float32 [4096, 4608], P('dp', 'tensor')
The draws below stay inside these ranges and needn't reach their ends.
Inputs may be any that keep to these rules, and one draw needn't show every extreme that they name: `example_user`: every user id occurs; user u occurs exactly user_counts[u] times. user_counts[u] counts the examples of user u; they sum to 32.
All inputs are finite; a program needn't handle non-finite values.
Results may differ from the reference program's by a relative error of at most 0.0008.
Values may be sent and summed in bfloat16 or wider, within the bound.
A program may use at most 128 MiB of HBM per device.

```python
import math
import jax
import jax.numpy as jnp
from jax import lax

D = 4608
HD = 4096
LEN = 1024
E_TOT = 32
USERS = 16
MOST = 4


def user_layout(key):
    key_heavy, key_order, key_shuffle = jax.random.split(key, 3)
    heavy = jax.random.randint(key_heavy, (), 0, USERS)
    order = jax.random.permutation(key_order, USERS)
    scores = jnp.where(order == heavy, USERS + 1, jnp.arange(USERS))
    others = order[jnp.argsort(scores, stable=True)].astype(jnp.int32)
    extra = jnp.concatenate([jnp.full((MOST - 1,), heavy, jnp.int32), others[:USERS - MOST + 1]])
    assigned = jnp.concatenate([jnp.arange(USERS, dtype=jnp.int32), extra])
    assigned = assigned[jax.random.permutation(key_shuffle, E_TOT)]
    tallies = jnp.sum((assigned[:, None] == jnp.arange(USERS, dtype=jnp.int32)[None, :]).astype(jnp.int32), axis=0)
    return (assigned, tallies)


def draw_example_user(key, part):
    assigned, tallies = user_layout(key)
    return assigned


def draw_user_counts(key, part):
    assigned, tallies = user_layout(key)
    return tallies


def draw_out_grad(key, part):
    key = jax.random.fold_in(key, 7)
    key_value, key_token, key_column, key_example = jax.random.split(key, 4)
    position = jnp.arange(E_TOT, dtype=jnp.float32) / max(E_TOT - 1, 1)
    values = jax.random.truncated_normal(key_value, -6.0, 6.0, (E_TOT, LEN, D), jnp.float32)
    token_scale = jnp.exp(jax.random.uniform(key_token, (E_TOT, LEN, 1), jnp.float32, 0.0, math.log(10.0)))
    token_rms = 4.64
    example_base = 0.25 * jnp.exp(position * math.log(3.0))
    column_ramp = 0.5 + jnp.arange(D, dtype=jnp.float32) / D
    column_scale = column_ramp * jnp.exp(jax.random.uniform(key_column, (D,), jnp.float32, 0.0, math.log(3.0)))
    example_scale = example_base * jnp.exp(jax.random.uniform(key_example, (E_TOT,), jnp.float32, 0.0, math.log(3.0)))
    result = values * token_scale * column_scale[None, None, :] * example_scale[:, None, None]
    return (result / (token_rms * math.sqrt(LEN))).astype(jnp.bfloat16)


def shard_levels(key, dims, pieces, low, largest):
    def one(dim, parts):
        steps = jax.random.uniform(jax.random.fold_in(jax.random.fold_in(key, 6), dim), (parts,), jnp.float32, low / len(pieces), largest / len(pieces))
        return jnp.repeat(jnp.exp(steps), dims[dim] // parts).reshape((-1,) + (1,) * (len(dims) - dim - 1))

    loudness = one(*pieces[0])
    for cut in pieces[1:]:
        loudness = loudness * one(*cut)
    return loudness


def centred(key, extent, spread, limit, cuts=(), kind=jnp.bfloat16):
    array = jax.random.normal(key, extent, jnp.float32) * spread
    if len(cuts) > 0:
        array = shard_levels(key, extent, cuts, -0.22, 0.18) * array
    return jnp.clip(array, min=-limit, max=limit).astype(kind)


def setup_inputs(seed: int = 0) -> dict:
    splits = jax.random.split(jax.random.key(seed), 5)
    return {
        "context": centred(splits[0], (E_TOT, LEN, HD), 1.0, 6.0, ((0, 16), (2, 16))),
        "out_grad": draw_out_grad(jax.random.fold_in(splits[4], 71), 0),
        "example_user": draw_example_user(jax.random.fold_in(splits[4], 71), 0),
        "user_counts": draw_user_counts(jax.random.fold_in(splits[4], 71), 0),
    }


def example_square(inputs):
    context_one, grad_one = inputs
    context_gram = jnp.dot(context_one, context_one.T, preferred_element_type=jnp.float32)
    grad_gram = jnp.dot(grad_one, grad_one.T, preferred_element_type=jnp.float32)
    return jnp.sum(context_gram * grad_gram)

def reference(context, out_grad, example_user, user_counts):
    squares = lax.map(example_square, (context, out_grad))
    example_norm = jnp.sqrt(squares + 1e-06)
    user_onehot = (example_user[:, None] == jnp.arange(USERS, dtype=jnp.int32)[None, :]).astype(jnp.float32)
    user_norm = lax.optimization_barrier(jnp.sum(example_norm[:, None] * user_onehot, axis=0))
    counts_float = user_counts.astype(jnp.float32)
    clip_bound = 1.5 * math.sqrt(HD * D)
    user_weight = jnp.minimum(1.0, clip_bound * counts_float / user_norm) / (counts_float * USERS)
    example_weight = lax.optimization_barrier(jnp.sum(user_onehot * user_weight[None, :], axis=1))

    def accumulate(total, inputs):
        context_one, grad_one, weight_one = inputs
        product = jnp.dot(context_one.T, grad_one, preferred_element_type=jnp.float32)
        return (total + weight_one * product, None)
    weight_grad = lax.scan(accumulate, jnp.zeros((HD, D), jnp.float32), (context, out_grad, example_weight))[0]
    return weight_grad
```

```python
import functools
import math

import jax
import jax.numpy as jnp
from jax import lax
from jax.experimental import pallas as pl
from jax.experimental.pallas import tpu as pltpu
from jax.sharding import PartitionSpec as P

MESH = pl.DeviceIdType.MESH
F32 = jnp.float32
SIDE = 4
RING = 8
GROUP = 16
STAGES = RING - 1


def kernel(clip_bound, context, grad, users, counts, out, held, grad_in, grad_t, terms, mask,
           squares, square_box, norm_box, first_box, group_box, second_box, last_box,
           local_sem, ring_send, ring_recv, side_send, square_send, square_recv,
           norm_send, norm_recv, sum_send, sum_recv):
    data, tensor = lax.axis_index("dp"), lax.axis_index("tensor")
    depth, core = lax.div(tensor, 2), lax.rem(tensor, 2)
    place = (lax.div(data, SIDE), lax.rem(data, SIDE))
    half = terms.shape[3] // 2

    def on_ring(step):
        return lax.rem(depth + step + RING, RING)

    right = (data, on_ring(1) * 2 + core)
    left = (data, on_ring(-1) * 2 + core)
    sibling = (data, depth * 2 + 1 - core)

    load_grad = pltpu.make_async_copy(grad, grad_in, local_sem.at[0])
    load_grad.start()
    load_own = pltpu.make_async_copy(context, held.at[tensor], local_sem.at[1])
    load_own.start()

    barrier = pltpu.get_barrier_semaphore()

    @pl.loop(1, GROUP)
    def _(step):
        pl.semaphore_signal(barrier, inc=1, device_id=(data, lax.rem(tensor + step, GROUP)), device_id_type=MESH)
        pl.semaphore_signal(barrier, inc=1, device_id=(lax.rem(data + step, GROUP), tensor), device_id_type=MESH)

    pl.semaphore_wait(barrier, 2 * (GROUP - 1))

    def chunk_copy(src, slot, example, send_sem, device):
        return pltpu.make_async_remote_copy(
            src_ref=src, dst_ref=held.at[slot, example], send_sem=send_sem,
            recv_sem=ring_recv.at[slot, example], device_id=device, device_id_type=MESH)

    for turn in range(2):
        chunk_copy(context.at[turn], tensor, turn, ring_send.at[0, turn], right).start()
        chunk_copy(context.at[1 - turn], tensor, 1 - turn, ring_send.at[1, turn], left).start()
    for turn in range(2):
        chunk_copy(context.at[turn], tensor, turn, side_send.at[0, turn], sibling).start()

    squares[...] = jnp.zeros_like(squares)
    load_grad.wait()
    for example in range(2):
        grad_t[example] = grad_in[example].T

    @pl.loop(0, 2 * GROUP)
    def _(item):
        for example in range(2):
            same = jnp.where(users[item] == users[2 * data + example], 1.0, 0.0)
            mask[example, item] = jnp.full(mask.shape[2:], same, F32)

    def product(slot, example):
        term = jnp.dot(grad_t[example], held[slot, example], preferred_element_type=F32)
        term = term.reshape(terms.shape[3:])
        terms[example, lax.div(slot, SIDE), lax.rem(slot, SIDE)] = term
        squares[example] += jnp.sum(term * term, axis=0)

    def arrived(slot, example):
        chunk_copy(context.at[0], slot, example, ring_send.at[0, 0], right).wait_recv()

    load_own.wait()
    for example in range(2):
        product(tensor, example)
    for example in range(2):
        arrived(depth * 2 + 1 - core, example)
        product(depth * 2 + 1 - core, example)

    @pl.loop(0, STAGES)
    def _(stage):
        distance = 1 + lax.div(stage, 2)
        turn = lax.rem(stage, 2)
        sources = ((on_ring(-distance), turn), (on_ring(distance), 1 - turn))
        for way, (source, example) in enumerate(sources):
            slot = source * 2 + core
            arrived(slot, example)

            @pl.when(stage < STAGES - 2)
            def _():
                chunk_copy(held.at[slot, example], slot, example, ring_send.at[way, 2 + stage],
                           (right, left)[way]).start()

            chunk_copy(held.at[slot, example], slot, example, side_send.at[way, 2 + stage], sibling).start()
        for source, example in sources:
            product(source * 2 + core, example)
        for source, example in sources:
            arrived(source * 2 + 1 - core, example)
            product(source * 2 + 1 - core, example)

    folded = squares[:, :, :128] + squares[:, :, 128:]
    square_box[tensor] = folded

    def square_copy(step):
        return pltpu.make_async_remote_copy(
            src_ref=square_box.at[tensor], dst_ref=square_box.at[tensor], send_sem=square_send.at[step],
            recv_sem=square_recv.at[tensor], device_id=(data, lax.rem(tensor + step, GROUP)), device_id_type=MESH)

    def square_arrival(step):
        peer = lax.rem(tensor + step, GROUP)
        return pltpu.make_async_remote_copy(
            src_ref=square_box.at[peer], dst_ref=square_box.at[peer], send_sem=square_send.at[step],
            recv_sem=square_recv.at[peer], device_id=(data, peer), device_id_type=MESH)

    @pl.loop(1, GROUP)
    def _(step):
        square_copy(step).start()

    @pl.loop(1, GROUP)
    def _(step):
        square_arrival(step).wait_recv()

    total = jnp.sum(square_box[...], axis=0)
    total = jnp.sum(jnp.sum(total, axis=2, keepdims=True), axis=1, keepdims=True)
    norm_box[data] = jnp.broadcast_to(jnp.sqrt(total + 1e-6), norm_box.shape[1:])

    def norm_copy(step):
        return pltpu.make_async_remote_copy(
            src_ref=norm_box.at[data], dst_ref=norm_box.at[data], send_sem=norm_send.at[step],
            recv_sem=norm_recv.at[data], device_id=(lax.rem(data + step, GROUP), tensor), device_id_type=MESH)

    def norm_arrival(step):
        peer = lax.rem(data + step, GROUP)
        return pltpu.make_async_remote_copy(
            src_ref=norm_box.at[peer], dst_ref=norm_box.at[peer], send_sem=norm_send.at[step],
            recv_sem=norm_recv.at[peer], device_id=(peer, tensor), device_id_type=MESH)

    @pl.loop(1, GROUP)
    def _(step):
        norm_copy(step).start()

    @pl.loop(1, GROUP)
    def _(step):
        norm_arrival(step).wait_recv()

    norms = norm_box[...].reshape((2 * GROUP,) + norm_box.shape[2:])
    weights = []
    for example in range(2):
        user_norm = jnp.sum(norms * mask[example], axis=0)
        count = counts[users[2 * data + example]].astype(F32)
        weight = jnp.minimum(1.0, clip_bound * count / user_norm) / (count * counts.shape[0])
        weights.append(jnp.concatenate([weight, weight], axis=1))

    def neighbour(dim, step):
        moved = list(place)
        moved[dim] = lax.rem(place[dim] + step + SIDE, SIDE)
        return (moved[0] * SIDE + moved[1], tensor)

    def along(dim, step):
        return lax.rem(place[dim] + step + SIDE, SIDE)

    def weighed(index):
        return weights[0] * terms[(0,) + index] + weights[1] * terms[(1,) + index]

    def spot(part, main, other, span):
        return (main, other, span) if part == 0 else (other, main, span)

    def sum_copy(part, phase, message, way, src, dst):
        number = ((part * 2 + phase) * 3 + message) * 2 + way
        dim = part if phase == 0 else 1 - part
        return pltpu.make_async_remote_copy(
            src_ref=src, dst_ref=dst, send_sem=sum_send.at[number], recv_sem=sum_recv.at[number],
            device_id=neighbour(dim, 1 if way == 0 else -1), device_id_type=MESH)

    pairs = (pl.ds(0, 2), pl.ds(2, 2))
    copies = []
    merges = []
    spans = (pl.ds(0, half), pl.ds(half, half))

    def send(*args):
        copy = sum_copy(*args)
        copy.start()
        copies.append(copy)
        return copy

    firsts, raws, joined = {}, {}, {}
    for part in range(2):
        for way in range(2):
            index = spot(part, along(part, 2), pairs[way], spans[part])
            terms[(0,) + index] = weighed(index)
            firsts[part, way] = send(part, 0, 0, way, terms.at[(0,) + index], first_box.at[part, way])
    for part in range(2):
        for way in range(2):
            index = spot(part, along(part, 1 if way == 0 else -1), pairs[1 - way], spans[part])
            terms[(0,) + index] = weighed(index)
            raws[part, way] = send(part, 0, 1, way, terms.at[(0,) + index], group_box.at[part, way, pairs[1 - way]])
    for part in range(2):
        for way in range(2):
            index = spot(part, along(part, 1 if way == 0 else -1), pairs[way], spans[part])
            firsts[part, way].wait_recv()
            terms[(0,) + index] = weighed(index) + first_box[part, way]
            joined[part, way] = send(part, 0, 2, way, terms.at[(0,) + index], group_box.at[part, way, pairs[way]])
    for part in range(2):
        for way in range(2):
            index = spot(part, place[part], pairs[way], spans[part])
            terms[(0,) + index] = weighed(index)
    for part in range(2):
        for way in range(2):
            raws[part, way].wait_recv()
            joined[part, way].wait_recv()
        index = spot(part, place[part], pl.ds(0, SIDE), spans[part])
        terms[(0,) + index] = terms[(0,) + index] + (group_box[part, 0] + group_box[part, 1])

    quarter = half // 2
    lows = (pl.ds(0, quarter), pl.ds(quarter, quarter))

    def piece(part, step, way):
        start = part * half + way * quarter
        return spot(part, place[part], along(1 - part, step), pl.ds(start, quarter))

    for part in range(2):
        for way in range(2):
            index = piece(part, 2, way)
            firsts[part, way] = send(part, 1, 0, way, terms.at[(0,) + index], second_box.at[part, way])
    for part in range(2):
        for way in range(2):
            index = piece(part, 1 if way == 0 else -1, 1 - way)
            raws[part, way] = send(part, 1, 1, way, terms.at[(0,) + index], last_box.at[part, way, lows[1 - way]])
    for part in range(2):
        for way in range(2):
            index = piece(part, 1 if way == 0 else -1, way)
            firsts[part, way].wait_recv()
            terms[(0,) + index] = terms[(0,) + index] + second_box[part, way]
            joined[part, way] = send(part, 1, 2, way, terms.at[(0,) + index], last_box.at[part, way, lows[way]])
    for part in range(2):
        for way in range(2):
            raws[part, way].wait_recv()
            joined[part, way].wait_recv()
        own = spot(part, place[part], place[1 - part], spans[part])
        out[spans[part]] = terms[(0,) + own] + (last_box[part, 0] + last_box[part, 1])

    for copy in copies:
        copy.wait_send()

    @pl.loop(1, GROUP)
    def _(step):
        square_copy(step).wait_send()
        norm_copy(step).wait_send()

    @pl.loop(0, STAGES)
    def _(stage):
        for way in range(2):
            @pl.when(stage < STAGES - 2)
            def _():
                chunk_copy(held.at[0, 0], 0, 0, ring_send.at[way, 2 + stage], right).wait_send()

            chunk_copy(held.at[0, 0], 0, 0, side_send.at[way, 2 + stage], sibling).wait_send()

    for turn in range(2):
        for way in range(2):
            chunk_copy(context.at[0], 0, 0, ring_send.at[way, turn], right).wait_send()
        chunk_copy(context.at[0], 0, 0, side_send.at[0, turn], sibling).wait_send()


def per_device(context, grad, users, counts):
    examples, length, width_in = context.shape
    width_out = grad.shape[2]
    tiles = width_out // 8
    half, quarter = tiles // 2, tiles // 4
    dma = pltpu.SemaphoreType.DMA
    vmem = pltpu.VMEM
    clip_bound = 1.5 * math.sqrt(width_in * width_out * GROUP * GROUP)
    flops = 2 * examples * length * width_in * width_out * GROUP
    result = pl.pallas_call(
        functools.partial(kernel, clip_bound),
        out_shape=jax.ShapeDtypeStruct((tiles, 8, width_in), F32),
        in_specs=[
            pl.BlockSpec(memory_space=pl.ANY),
            pl.BlockSpec(memory_space=pl.ANY),
            pl.BlockSpec(memory_space=pltpu.SMEM),
            pl.BlockSpec(memory_space=pltpu.SMEM),
        ],
        out_specs=pl.BlockSpec(memory_space=pltpu.VMEM),
        scratch_shapes=[
            vmem((GROUP, examples, length, width_in), context.dtype),
            vmem((examples, length, width_out), grad.dtype),
            vmem((examples, width_out, length), grad.dtype),
            vmem((examples, SIDE, SIDE, tiles, 8, width_in), F32),
            vmem((examples, 2 * GROUP, 8, 128), F32),
            vmem((examples, 8, width_in), F32),
            vmem((GROUP, examples, 8, 128), F32),
            vmem((GROUP, examples, 8, 128), F32),
            vmem((2, 2, 2, half, 8, width_in), F32),
            vmem((2, 2, SIDE, half, 8, width_in), F32),
            vmem((2, 2, quarter, 8, width_in), F32),
            vmem((2, 2, half, 8, width_in), F32),
            dma((2,)),
            dma((2, 2 + STAGES)),
            dma((GROUP, 2)),
            dma((2, 2 + STAGES)),
            dma((GROUP,)),
            dma((GROUP,)),
            dma((GROUP,)),
            dma((GROUP,)),
            dma((24,)),
            dma((24,)),
        ],
        compiler_params=pltpu.CompilerParams(
            collective_id=0, has_side_effects=True, vmem_limit_bytes=56 * 2**20),
        cost_estimate=pl.CostEstimate(flops=flops, bytes_accessed=2 * context.size + 2 * grad.size, transcendentals=0),
    )(context, grad, users, counts)
    return result.reshape(width_out, width_in).T


def solution(mesh):
    in_specs = (P("dp", None, "tensor"), P("dp", None, "tensor"), P(), P())
    out_specs = P("dp", "tensor")
    return jax.shard_map(
        per_device, mesh=mesh, in_specs=in_specs, out_specs=out_specs, check_vma=False
    )
```

```python
import functools
import math

import jax
import jax.numpy as jnp
from jax import lax
from jax.experimental import pallas as pl
from jax.experimental.pallas import tpu as pltpu
from jax.sharding import PartitionSpec as P

MESH = pl.DeviceIdType.MESH
F32 = jnp.float32
SIDE = 4
RING = 8
GROUP = 16
STAGES = RING - 1
STEPS = 32000.0
FIRST_UNITS = 9


def kernel(clip_bound, context, grad, users, counts, out, held, grad_t, terms, coded_x, coded_y, early_x, early_y,
           same_user, user_count, weight, squares, square_box, norm_box, sum_x, sum_y, second_x, second_y, last_x, last_y,
           local_sem, ring_send, ring_recv, side_send, early_send, early_recv, square_send, square_recv,
           norm_send, norm_recv, sum_send, sum_recv):
    data, tensor = lax.axis_index("dp"), lax.axis_index("tensor")
    depth, core = lax.div(tensor, 2), lax.rem(tensor, 2)
    place = (lax.div(data, SIDE), lax.rem(data, SIDE))
    coded, early = (coded_x, coded_y), (early_x, early_y)
    sums, second, last = (sum_x, sum_y), (second_x, second_y), (last_x, last_y)
    units = (coded_x.shape[2] - 1, coded_y.shape[2] - 1)
    starts = (0, units[0])

    def on_ring(step):
        return lax.rem(depth + step + RING, RING)

    right = (data, on_ring(1) * 2 + core)
    left = (data, on_ring(-1) * 2 + core)
    sibling = (data, depth * 2 + 1 - core)

    load_grad = pltpu.make_async_copy(grad, grad_t, local_sem.at[0])
    load_grad.start()
    load_own = pltpu.make_async_copy(context, held.at[tensor], local_sem.at[1])
    load_own.start()

    barrier = pltpu.get_barrier_semaphore()

    @pl.loop(1, GROUP)
    def _(step):
        pl.semaphore_signal(barrier, inc=1, device_id=(data, lax.rem(tensor + step, GROUP)), device_id_type=MESH)
        pl.semaphore_signal(barrier, inc=1, device_id=(lax.rem(data + step, GROUP), tensor), device_id_type=MESH)

    pl.semaphore_wait(barrier, 2 * (GROUP - 1))

    def chunk_copy(src, slot, example, send_sem, device):
        return pltpu.make_async_remote_copy(
            src_ref=src, dst_ref=held.at[slot, example], send_sem=send_sem,
            recv_sem=ring_recv.at[slot, example], device_id=device, device_id_type=MESH)

    for turn in range(2):
        chunk_copy(context.at[turn], tensor, turn, ring_send.at[0, turn], right).start()
        chunk_copy(context.at[1 - turn], tensor, 1 - turn, ring_send.at[1, turn], left).start()
    for turn in range(2):
        chunk_copy(context.at[turn], tensor, turn, side_send.at[0, turn], sibling).start()

    squares[...] = jnp.zeros_like(squares)
    lanes = lax.broadcasted_iota(jnp.int32, (1, 128), 1)
    everyone = jnp.full((1, 128), -1, jnp.int32)
    for item in range(2 * GROUP):
        everyone = jnp.where(lanes == item, users[item], everyone)

    @pl.loop(0, 2 * GROUP)
    def _(item):
        same_user[item] = jnp.where(everyone == users[item], 1.0, 0.0)
        user_count[item] = jnp.full((1, 128), counts[users[item]].astype(F32), F32)

    load_grad.wait()

    def early_copy(part, slot, example):
        spot = (lax.div(slot, SIDE), lax.rem(slot, SIDE))
        owner = (spot[0] * SIDE + place[1], tensor) if part == 0 else (place[0] * SIDE + spot[1], tensor)
        return pltpu.make_async_remote_copy(
            src_ref=coded[part].at[slot, example], dst_ref=early[part].at[place[part], example, spot[1 - part]],
            send_sem=early_send.at[part], recv_sem=early_recv.at[part], device_id=owner, device_id_type=MESH)

    def product(slot, example):
        term = jnp.dot(grad_t[example], held[slot, example], preferred_element_type=F32)
        tiles = term.reshape(terms.shape[3:])
        spot = (lax.div(slot, SIDE), lax.rem(slot, SIDE))
        terms[example, spot[0], spot[1]] = tiles
        squares[example] += jnp.sum(tiles * tiles, axis=0)
        peak = jnp.max(jnp.max(jnp.abs(tiles), axis=0), axis=0, keepdims=True)
        power = jnp.ceil(jnp.log2(jnp.maximum(peak, 1e-30)))
        steps = jnp.round(term * (STEPS * jnp.exp2(-power))).astype(jnp.int32).astype(jnp.int16)
        steps = steps.reshape((sum(units), 16) + steps.shape[1:])
        powers = jnp.broadcast_to(power, (16,) + power.shape[1:]).astype(jnp.int32).astype(jnp.int16)
        for part in range(2):
            coded[part][slot, example, 0:units[part]] = steps[starts[part]:starts[part] + units[part]]
            coded[part][slot, example, units[part]] = powers

            @pl.when(spot[part] != place[part])
            def _():
                early_copy(part, slot, example).start()

    def arrived(slot, example):
        chunk_copy(context.at[0], slot, example, ring_send.at[0, 0], right).wait_recv()

    load_own.wait()
    for example in range(2):
        product(tensor, example)
    for example in range(2):
        arrived(depth * 2 + 1 - core, example)
        product(depth * 2 + 1 - core, example)

    @pl.loop(0, STAGES)
    def _(stage):
        distance = 1 + lax.div(stage, 2)
        turn = lax.rem(stage, 2)
        sources = ((on_ring(-distance), turn), (on_ring(distance), 1 - turn))
        for way, (source, example) in enumerate(sources):
            slot = source * 2 + core
            arrived(slot, example)

            @pl.when(stage < STAGES - 2)
            def _():
                chunk_copy(held.at[slot, example], slot, example, ring_send.at[way, 2 + stage],
                           (right, left)[way]).start()

            chunk_copy(held.at[slot, example], slot, example, side_send.at[way, 2 + stage], sibling).start()
        for source, example in sources:
            product(source * 2 + core, example)
        for source, example in sources:
            arrived(source * 2 + 1 - core, example)
            product(source * 2 + 1 - core, example)

    lanes = lax.broadcasted_iota(jnp.int32, (8, 128), 1)

    def in_lanes(values):
        return jnp.where(lanes == 2 * data, values[0], jnp.where(lanes == 2 * data + 1, values[1], 0.0))

    own = [jnp.sum(jnp.sum(squares[example], axis=1, keepdims=True), axis=0, keepdims=True) for example in range(2)]
    square_box[tensor] = in_lanes(own)

    def square_copy(step):
        return pltpu.make_async_remote_copy(
            src_ref=square_box.at[tensor], dst_ref=square_box.at[tensor], send_sem=square_send.at[step],
            recv_sem=square_recv.at[tensor], device_id=(data, lax.rem(tensor + step, GROUP)), device_id_type=MESH)

    def square_arrival(step):
        peer = lax.rem(tensor + step, GROUP)
        return pltpu.make_async_remote_copy(
            src_ref=square_box.at[peer], dst_ref=square_box.at[peer], send_sem=square_send.at[step],
            recv_sem=square_recv.at[peer], device_id=(data, peer), device_id_type=MESH)

    @pl.loop(1, GROUP)
    def _(step):
        square_copy(step).start()

    @pl.loop(1, GROUP)
    def _(step):
        square_arrival(step).wait_recv()

    norm = jnp.sqrt(jnp.sum(square_box[...], axis=0) + 1e-6)
    norm_box[data] = in_lanes((norm, norm))

    def norm_copy(step):
        return pltpu.make_async_remote_copy(
            src_ref=norm_box.at[data], dst_ref=norm_box.at[data], send_sem=norm_send.at[step],
            recv_sem=norm_recv.at[data], device_id=(lax.rem(data + step, GROUP), tensor), device_id_type=MESH)

    def norm_arrival(step):
        peer = lax.rem(data + step, GROUP)
        return pltpu.make_async_remote_copy(
            src_ref=norm_box.at[peer], dst_ref=norm_box.at[peer], send_sem=norm_send.at[step],
            recv_sem=norm_recv.at[peer], device_id=(peer, tensor), device_id_type=MESH)

    @pl.loop(1, GROUP)
    def _(step):
        norm_copy(step).start()

    @pl.loop(1, GROUP)
    def _(step):
        norm_arrival(step).wait_recv()

    norms = jnp.sum(norm_box[...], axis=0)[0:1]
    user_norm = jnp.sum(same_user[...] * norms, axis=2, keepdims=True)
    count = user_count[...]
    weight[...] = jnp.minimum(1.0, clip_bound * count / user_norm) / (count * counts.shape[0])

    def wide(row):
        return jnp.concatenate([row, row], axis=1)

    def along(dim, step):
        return lax.rem(place[dim] + step + SIDE, SIDE)

    def at(dim, value):
        return value * SIDE + place[1] if dim == 0 else place[0] * SIDE + value

    def gathered(part, other):
        spot = (place[0], other) if part == 0 else (other, place[1])
        span = pl.ds(2 * starts[part], 2 * units[part])
        total = sum(wide(weight[2 * data + example]) * terms[(example,) + spot + (span,)] for example in range(2))
        for step in range(1, SIDE):
            source = along(part, step)
            for example in range(2):
                block = early[part].at[source, example, other]
                power = block[units[part]].astype(jnp.int32).astype(F32)[0:1]
                scale = wide(weight[2 * at(part, source) + example]) * (jnp.exp2(power) * (1.0 / STEPS))
                steps = block[0:units[part]].astype(jnp.int32).astype(F32)
                total = total + scale * steps.reshape(total.shape)
        return total

    def sum_copy(part, message, way, src, dst):
        number = (part * 3 + message) * 2 + way
        dim = 1 - part
        return pltpu.make_async_remote_copy(
            src_ref=src, dst_ref=dst, send_sem=sum_send.at[number], recv_sem=sum_recv.at[number],
            device_id=(at(dim, along(dim, 1 if way == 0 else -1)), tensor), device_id_type=MESH)

    copies = []

    def send(*args):
        copy = sum_copy(*args)
        copy.start()
        copies.append(copy)
        return copy

    lows = tuple((pl.ds(0, count), pl.ds(count, count)) for count in units)
    firsts, raws, joined = {}, {}, {}
    for part in range(2):
        pltpu.make_async_remote_copy(
            src_ref=early[part].at[pl.ds(0, SIDE - 1)], dst_ref=early[part].at[pl.ds(0, SIDE - 1)],
            send_sem=early_send.at[part], recv_sem=early_recv.at[part], device_id=sibling, device_id_type=MESH).wait_recv()
    for part in range(2):
        other = along(1 - part, 2)
        sums[part][other] = gathered(part, other)
        for way in range(2):
            firsts[part, way] = send(part, 0, way, sums[part].at[other, lows[part][way]], second[part].at[way])
    for part in range(2):
        for way in range(2):
            other = along(1 - part, 1 if way == 0 else -1)
            sums[part][other] = gathered(part, other)
            span = lows[part][1 - way]
            raws[part, way] = send(part, 1, way, sums[part].at[other, span], last[part].at[way, span])
    for part in range(2):
        for way in range(2):
            other = along(1 - part, 1 if way == 0 else -1)
            span = lows[part][way]
            firsts[part, way].wait_recv()
            sums[part][other, span] = sums[part][other, span] + second[part][way]
            joined[part, way] = send(part, 2, way, sums[part].at[other, span], last[part].at[way, span])
    for part in range(2):
        sums[part][place[1 - part]] = gathered(part, place[1 - part])
    for part in range(2):
        for way in range(2):
            raws[part, way].wait_recv()
            joined[part, way].wait_recv()
        out[pl.ds(2 * starts[part], 2 * units[part])] = sums[part][place[1 - part]] + (last[part][0] + last[part][1])

    for copy in copies:
        copy.wait_send()
    for part in range(2):
        pltpu.make_async_remote_copy(
            src_ref=early[part].at[pl.ds(0, SIDE - 1)], dst_ref=early[part].at[pl.ds(0, SIDE - 1)],
            send_sem=early_send.at[part], recv_sem=early_recv.at[part], device_id=sibling, device_id_type=MESH).wait_send()

    @pl.loop(1, GROUP)
    def _(step):
        square_copy(step).wait_send()
        norm_copy(step).wait_send()

    @pl.loop(0, STAGES)
    def _(stage):
        for way in range(2):
            @pl.when(stage < STAGES - 2)
            def _():
                chunk_copy(held.at[0, 0], 0, 0, ring_send.at[way, 2 + stage], right).wait_send()

            chunk_copy(held.at[0, 0], 0, 0, side_send.at[way, 2 + stage], sibling).wait_send()

    for turn in range(2):
        for way in range(2):
            chunk_copy(context.at[0], 0, 0, ring_send.at[way, turn], right).wait_send()
        chunk_copy(context.at[0], 0, 0, side_send.at[0, turn], sibling).wait_send()


def per_device(context, grad, users, counts):
    examples, length, width_in = context.shape
    width_out = grad.shape[2]
    tiles = width_out // 8
    units = (FIRST_UNITS, width_out // 16 - FIRST_UNITS)
    dma = pltpu.SemaphoreType.DMA
    vmem = pltpu.VMEM
    clip_bound = 1.5 * math.sqrt(width_in * width_out * GROUP * GROUP)
    flops = 2 * examples * length * width_in * width_out * GROUP
    result = pl.pallas_call(
        functools.partial(kernel, clip_bound),
        out_shape=jax.ShapeDtypeStruct((tiles, 8, width_in), F32),
        in_specs=[
            pl.BlockSpec(memory_space=pl.ANY),
            pl.BlockSpec(memory_space=pl.ANY),
            pl.BlockSpec(memory_space=pltpu.SMEM),
            pl.BlockSpec(memory_space=pltpu.SMEM),
        ],
        out_specs=pl.BlockSpec(memory_space=pltpu.VMEM),
        scratch_shapes=[
            vmem((GROUP, examples, length, width_in), context.dtype),
            vmem((examples, width_out, length), grad.dtype),
            vmem((examples, SIDE, SIDE, tiles, 8, width_in), F32),
            *(vmem((GROUP, examples, count + 1, 16, width_in), jnp.int16) for count in units),
            *(vmem((SIDE, examples, SIDE, count + 1, 16, width_in), jnp.int16) for count in units),
            vmem((2 * GROUP, 1, 128), F32),
            vmem((2 * GROUP, 1, 128), F32),
            vmem((2 * GROUP, 1, 128), F32),
            vmem((examples, 8, width_in), F32),
            vmem((GROUP, 8, 128), F32),
            vmem((GROUP, 8, 128), F32),
            *(vmem((SIDE, 2 * count, 8, width_in), F32) for count in units),
            *(vmem((2, count, 8, width_in), F32) for count in units),
            *(vmem((2, 2 * count, 8, width_in), F32) for count in units),
            dma((2,)),
            dma((2, 2 + STAGES)),
            dma((GROUP, 2)),
            dma((2, 2 + STAGES)),
            dma((2,)),
            dma((2,)),
            dma((GROUP,)),
            dma((GROUP,)),
            dma((GROUP,)),
            dma((GROUP,)),
            dma((12,)),
            dma((12,)),
        ],
        compiler_params=pltpu.CompilerParams(
            collective_id=0, has_side_effects=True, vmem_limit_bytes=56 * 2**20),
        cost_estimate=pl.CostEstimate(flops=flops, bytes_accessed=2 * context.size + 2 * grad.size, transcendentals=0),
    )(context, jnp.swapaxes(grad, 1, 2), users, counts)
    return result.reshape(width_out, width_in).T


def solution(mesh):
    in_specs = (P("dp", None, "tensor"), P("dp", None, "tensor"), P(), P())
    out_specs = P("dp", "tensor")
    return jax.shard_map(
        per_device, mesh=mesh, in_specs=in_specs, out_specs=out_specs, check_vma=False
    )
```

```python
import functools
import math

import jax
import jax.numpy as jnp
from jax import lax
from jax.experimental import pallas as pl
from jax.experimental.pallas import tpu as pltpu
from jax.sharding import PartitionSpec as P

MESH = pl.DeviceIdType.MESH
F32 = jnp.float32
SIDE = 4
RING = 8
GROUP = 16
LANES = 128
HALVES = 2
PIECES = 2 * HALVES
STAGES = (RING // 2 - 1) * PIECES + HALVES
FORWARDS = STAGES - PIECES
STEPS = 32000.0
FIRST_UNITS = 9
FAR_TENSOR = sorted(range(1, GROUP), key=lambda step: -min(step, GROUP - step))
FAR_DATA = sorted(range(1, GROUP), key=lambda step: -min(step // SIDE, SIDE - step // SIDE) - min(step % SIDE, SIDE - step % SIDE))


def encode(tiles):
    peak = jnp.max(jnp.max(jnp.abs(tiles), axis=0), axis=0, keepdims=True)
    power = jnp.ceil(jnp.log2(jnp.maximum(peak, 1e-30)))
    steps = jnp.round(tiles * (STEPS * jnp.exp2(-power))[None]).astype(jnp.int32).astype(jnp.int16)
    powers = jnp.broadcast_to(power, (16,) + power.shape[1:]).astype(jnp.int32).astype(jnp.int16)
    return steps.reshape((tiles.shape[0] // 2, 16) + tiles.shape[2:]), powers


def decode(ref, factor):
    units = ref.shape[0] - 1
    power = ref[units].astype(jnp.int32).astype(F32)[0:1]
    scale = factor * (jnp.exp2(power) * (1.0 / STEPS))
    steps = ref[0:units].astype(jnp.int32).astype(F32)
    return scale * steps.reshape((2 * units, 8) + ref.shape[2:])


def kernel(clip_bound, context, grad, users, counts, out, held, grad_t, terms, coded_x, coded_y, early_x, early_y,
           same_user, user_count, weight, squares, square_box, norm_box, late_x, late_y, final_x, final_y,
           local_sem, ring_send, ring_recv, side_send, early_send, early_recv, square_send, square_recv,
           norm_send, norm_recv, sum_send, sum_recv, hello):
    data, tensor = lax.axis_index("dp"), lax.axis_index("tensor")
    depth, core = lax.div(tensor, 2), lax.rem(tensor, 2)
    place = (lax.div(data, SIDE), lax.rem(data, SIDE))
    coded, early = (coded_x, coded_y), (early_x, early_y)
    late, final = (late_x, late_y), (final_x, final_y)
    units = (coded_x.shape[3] - 1, coded_y.shape[3] - 1)
    starts = (0, units[0])

    def on_ring(step):
        return lax.rem(depth + step + RING, RING)

    def along(dim, step):
        return lax.rem(place[dim] + step + SIDE, SIDE)

    def at(dim, value):
        return value * SIDE + place[1] if dim == 0 else place[0] * SIDE + value

    right = (data, on_ring(1) * 2 + core)
    left = (data, on_ring(-1) * 2 + core)
    sibling = (data, depth * 2 + 1 - core)
    around = tuple((at(dim, along(dim, step)), tensor) for dim in range(2) for step in (1, -1))

    barrier = pltpu.get_barrier_semaphore()
    for device in (right, left) + around + (sibling,):
        pl.semaphore_signal(barrier, inc=1, device_id=device, device_id_type=MESH)

    load_grad = pltpu.make_async_copy(grad, grad_t, local_sem.at[0])
    loads = []
    for example in range(2):
        for part in range(HALVES):
            loads.append(pltpu.make_async_copy(
                context.at[example, :, pl.ds(part * LANES, LANES)], held.at[tensor, example, part],
                local_sem.at[1 + example * HALVES + part]))
    for copy in loads:
        copy.start()
    load_grad.start()
    for copy in loads:
        copy.wait()

    pl.semaphore_wait(barrier, 7)

    def chunk_copy(slot, example, part, send_sem, device):
        return pltpu.make_async_remote_copy(
            src_ref=held.at[slot, example, part], dst_ref=held.at[slot, example, part], send_sem=send_sem,
            recv_sem=ring_recv.at[slot, example, part], device_id=device, device_id_type=MESH)

    for piece in range(PIECES):
        turn, part = piece // HALVES, piece % HALVES
        chunk_copy(tensor, turn, part, ring_send.at[0, piece], right).start()
        chunk_copy(tensor, 1 - turn, part, ring_send.at[1, piece], left).start()
    for piece in range(PIECES):
        chunk_copy(tensor, piece // HALVES, piece % HALVES, side_send.at[0, piece], sibling).start()

    for turn in range(3):
        for device in around:
            pl.semaphore_signal(hello.at[turn], inc=1, device_id=device, device_id_type=MESH)
        pl.semaphore_wait(hello.at[turn], 4)

    squares[...] = jnp.zeros_like(squares)
    lanes = lax.broadcasted_iota(jnp.int32, (1, LANES), 1)
    everyone = jnp.full((1, LANES), -1, jnp.int32)
    for item in range(2 * GROUP):
        everyone = jnp.where(lanes == item, users[item], everyone)

    @pl.loop(0, 2 * GROUP)
    def _(item):
        same_user[item] = jnp.where(everyone == users[item], 1.0, 0.0)
        user_count[item] = jnp.full((1, LANES), counts[users[item]].astype(F32), F32)

    load_grad.wait()

    def early_copy(dim, slot, example, part):
        spot = (lax.div(slot, SIDE), lax.rem(slot, SIDE))
        return pltpu.make_async_remote_copy(
            src_ref=coded[dim].at[slot, example, part], dst_ref=early[dim].at[place[dim], example, spot[1 - dim], part],
            send_sem=early_send.at[dim], recv_sem=early_recv.at[dim], device_id=(at(dim, spot[dim]), tensor),
            device_id_type=MESH)

    def product(slot, example, part):
        term = jnp.dot(grad_t[example], held[slot, example, part], preferred_element_type=F32)
        tiles = term.reshape(terms.shape[4:])
        spot = (lax.div(slot, SIDE), lax.rem(slot, SIDE))
        terms[example, spot[0], spot[1], part] = tiles
        squares[example] += jnp.sum(tiles * tiles, axis=0)
        steps, powers = encode(tiles)
        for dim in range(2):
            coded[dim][slot, example, part, 0:units[dim]] = steps[starts[dim]:starts[dim] + units[dim]]
            coded[dim][slot, example, part, units[dim]] = powers

            @pl.when(spot[dim] != place[dim])
            def _():
                early_copy(dim, slot, example, part).start()

    def arrived(slot, example, part):
        chunk_copy(slot, example, part, ring_send.at[0, 0], right).wait_recv()

    @pl.loop(0, PIECES)
    def _(piece):
        product(tensor, lax.div(piece, HALVES), lax.rem(piece, HALVES))

    @pl.loop(0, PIECES)
    def _(piece):
        example, part = lax.div(piece, HALVES), lax.rem(piece, HALVES)
        arrived(depth * 2 + 1 - core, example, part)
        product(depth * 2 + 1 - core, example, part)

    @pl.loop(0, STAGES)
    def _(stage):
        distance = 1 + lax.div(stage, PIECES)
        turn = lax.div(lax.rem(stage, PIECES), HALVES)
        part = lax.rem(stage, HALVES)
        sources = ((on_ring(-distance), turn), (on_ring(distance), 1 - turn))
        for way, (source, example) in enumerate(sources):
            slot = source * 2 + core
            arrived(slot, example, part)

            @pl.when(stage < FORWARDS)
            def _():
                chunk_copy(slot, example, part, ring_send.at[way, PIECES + stage], (right, left)[way]).start()

            chunk_copy(slot, example, part, side_send.at[way, PIECES + stage], sibling).start()
        for source, example in sources:
            product(source * 2 + core, example, part)
        for source, example in sources:
            arrived(source * 2 + 1 - core, example, part)
            product(source * 2 + 1 - core, example, part)

    lanes = lax.broadcasted_iota(jnp.int32, (8, LANES), 1)

    def in_lanes(values):
        return jnp.where(lanes == 2 * data, values[0], jnp.where(lanes == 2 * data + 1, values[1], 0.0))

    own = [jnp.sum(jnp.sum(squares[example], axis=0, keepdims=True), axis=1, keepdims=True) for example in range(2)]
    square_box[tensor] = in_lanes(own)

    def square_copy(step, index):
        return pltpu.make_async_remote_copy(
            src_ref=square_box.at[tensor], dst_ref=square_box.at[tensor], send_sem=square_send.at[step],
            recv_sem=square_recv.at[index], device_id=(data, lax.rem(tensor + step, GROUP)), device_id_type=MESH)

    for step in FAR_TENSOR:
        square_copy(step, tensor).start()
    for step in reversed(FAR_TENSOR):
        square_copy(step, lax.rem(tensor + step, GROUP)).wait_recv()

    norm = jnp.sqrt(jnp.sum(square_box[...], axis=0) + 1e-6)
    norm_box[data] = in_lanes((norm, norm))

    def norm_copy(step, index):
        peer = lax.rem(place[0] + step // SIDE, SIDE) * SIDE + lax.rem(place[1] + step % SIDE, SIDE)
        return pltpu.make_async_remote_copy(
            src_ref=norm_box.at[data], dst_ref=norm_box.at[data], send_sem=norm_send.at[step],
            recv_sem=norm_recv.at[peer if index is None else index], device_id=(peer, tensor), device_id_type=MESH)

    for step in FAR_DATA:
        norm_copy(step, data).start()
    for step in reversed(FAR_DATA):
        norm_copy(step, None).wait_recv()

    norms = jnp.sum(norm_box[...], axis=0)[0:1]
    user_norm = jnp.sum(same_user[...] * norms, axis=2, keepdims=True)
    count = user_count[...]
    weight[...] = jnp.minimum(1.0, clip_bound * count / user_norm) / (count * counts.shape[0])

    def all_early(dim):
        whole = early[dim].at[pl.ds(0, SIDE - 1)]
        return pltpu.make_async_remote_copy(
            src_ref=whole, dst_ref=whole, send_sem=early_send.at[dim], recv_sem=early_recv.at[dim],
            device_id=sibling, device_id_type=MESH)

    def gathered(dim, other, part):
        spot = (place[0], other) if dim == 0 else (other, place[1])
        span = pl.ds(2 * starts[dim], 2 * units[dim])
        total = sum(weight[2 * data + example] * terms[(example,) + spot + (part, span)] for example in range(2))
        for step in range(1, SIDE):
            source = along(dim, step)
            for example in range(2):
                total = total + decode(early[dim].at[source, example, other, part], weight[2 * at(dim, source) + example])
        return total

    def sum_copy(dim, step):
        return pltpu.make_async_remote_copy(
            src_ref=late[dim].at[step - 1], dst_ref=final[dim].at[step - 1], send_sem=sum_send.at[dim, step - 1],
            recv_sem=sum_recv.at[dim, step - 1], device_id=(at(1 - dim, along(1 - dim, step)), tensor),
            device_id_type=MESH)

    for dim in range(2):
        all_early(dim).wait_recv()
    for step in (2, 1, 3):
        for dim in range(2):
            for part in range(HALVES):
                steps, powers = encode(gathered(dim, along(1 - dim, step), part))
                late[dim][step - 1, part, 0:units[dim]] = steps
                late[dim][step - 1, part, units[dim]] = powers
            sum_copy(dim, step).start()
    own = {}
    for dim in range(2):
        for part in range(HALVES):
            span = pl.ds(2 * starts[dim], 2 * units[dim])
            out[span, :, pl.ds(part * LANES, LANES)] = gathered(dim, place[1 - dim], part)
    for step in (1, 3, 2):
        for dim in range(2):
            sum_copy(dim, step).wait_recv()
            for part in range(HALVES):
                span = pl.ds(2 * starts[dim], 2 * units[dim])
                out[span, :, pl.ds(part * LANES, LANES)] += decode(final[dim].at[step - 1, part], 1.0)

    for dim in range(2):
        for step in range(1, SIDE):
            sum_copy(dim, step).wait_send()
        all_early(dim).wait_send()
    for step in range(1, GROUP):
        square_copy(step, tensor).wait_send()
        norm_copy(step, data).wait_send()

    @pl.loop(0, PIECES + STAGES)
    def _(index):
        for way in range(2):
            @pl.when(index < PIECES + FORWARDS)
            def _():
                chunk_copy(0, 0, 0, ring_send.at[way, index], right).wait_send()

            if way == 0:
                chunk_copy(0, 0, 0, side_send.at[way, index], sibling).wait_send()
            else:
                @pl.when(index >= PIECES)
                def _():
                    chunk_copy(0, 0, 0, side_send.at[way, index], sibling).wait_send()


def per_device(context, grad, users, counts):
    examples, length, width_in = context.shape
    width_out = grad.shape[2]
    tiles = width_out // 8
    units = (FIRST_UNITS, width_out // 16 - FIRST_UNITS)
    dma = pltpu.SemaphoreType.DMA
    vmem = pltpu.VMEM
    int16 = jnp.int16
    clip_bound = 1.5 * math.sqrt(width_in * width_out * GROUP * GROUP)
    flops = 2 * examples * length * width_in * width_out * GROUP
    result = pl.pallas_call(
        functools.partial(kernel, clip_bound),
        out_shape=jax.ShapeDtypeStruct((tiles, 8, width_in), F32),
        in_specs=[
            pl.BlockSpec(memory_space=pl.ANY),
            pl.BlockSpec(memory_space=pl.ANY),
            pl.BlockSpec(memory_space=pltpu.SMEM),
            pl.BlockSpec(memory_space=pltpu.SMEM),
        ],
        out_specs=pl.BlockSpec(memory_space=pltpu.VMEM),
        scratch_shapes=[
            vmem((GROUP, examples, HALVES, length, LANES), context.dtype),
            vmem((examples, width_out, length), grad.dtype),
            vmem((examples, SIDE, SIDE, HALVES, tiles, 8, LANES), F32),
            *(vmem((GROUP, examples, HALVES, count + 1, 16, LANES), int16) for count in units),
            *(vmem((SIDE, examples, SIDE, HALVES, count + 1, 16, LANES), int16) for count in units),
            vmem((2 * GROUP, 1, LANES), F32),
            vmem((2 * GROUP, 1, LANES), F32),
            vmem((2 * GROUP, 1, LANES), F32),
            vmem((examples, 8, LANES), F32),
            vmem((GROUP, 8, LANES), F32),
            vmem((GROUP, 8, LANES), F32),
            *(vmem((SIDE - 1, HALVES, count + 1, 16, LANES), int16) for count in units),
            *(vmem((SIDE - 1, HALVES, count + 1, 16, LANES), int16) for count in units),
            dma((1 + PIECES,)),
            dma((2, PIECES + STAGES)),
            dma((GROUP, 2, HALVES)),
            dma((2, PIECES + STAGES)),
            dma((2,)),
            dma((2,)),
            dma((GROUP,)),
            dma((GROUP,)),
            dma((GROUP,)),
            dma((GROUP,)),
            dma((2, SIDE - 1)),
            dma((2, SIDE - 1)),
            pltpu.SemaphoreType.REGULAR((3,)),
        ],
        compiler_params=pltpu.CompilerParams(
            collective_id=0, has_side_effects=True, vmem_limit_bytes=56 * 2**20),
        cost_estimate=pl.CostEstimate(flops=flops, bytes_accessed=2 * context.size + 2 * grad.size, transcendentals=0),
    )(context, jnp.swapaxes(grad, 1, 2), users, counts)
    return result.reshape(width_out, width_in).T


def solution(mesh):
    in_specs = (P("dp", None, "tensor"), P("dp", None, "tensor"), P(), P())
    out_specs = P("dp", "tensor")
    return jax.shard_map(
        per_device, mesh=mesh, in_specs=in_specs, out_specs=out_specs, check_vma=False
    )
```

```python
import functools
import math

import jax
import jax.numpy as jnp
from jax import lax
from jax.experimental import pallas as pl
from jax.experimental.pallas import tpu as pltpu
from jax.sharding import PartitionSpec as P

MESH = pl.DeviceIdType.MESH
F32 = jnp.float32
SIDE = 4
RING = 8
GROUP = 16
LANES = 128
HALVES = 2
PIECES = 2 * HALVES
STAGES = (RING // 2 - 1) * PIECES + HALVES
FORWARDS = STAGES - PIECES
STEPS = 32000.0
FIRST_UNITS = 9
FAR_TENSOR = sorted(range(1, GROUP), key=lambda step: -min(step, GROUP - step))
FAR_DATA = sorted(range(1, GROUP), key=lambda step: -min(step // SIDE, SIDE - step // SIDE) - min(step % SIDE, SIDE - step % SIDE))


def encode(tiles):
    peak = jnp.max(jnp.max(jnp.abs(tiles), axis=0), axis=0, keepdims=True)
    power = jnp.ceil(jnp.log2(jnp.maximum(peak, 1e-30)))
    steps = jnp.round(tiles * (STEPS * jnp.exp2(-power))[None]).astype(jnp.int32).astype(jnp.int16)
    powers = jnp.broadcast_to(power, (16,) + power.shape[1:]).astype(jnp.int32).astype(jnp.int16)
    return steps.reshape((tiles.shape[0] // 2, 16) + tiles.shape[2:]), powers


def decode(ref, factor):
    units = ref.shape[0] - 1
    power = ref[units].astype(jnp.int32).astype(F32)[0:1]
    scale = factor * (jnp.exp2(power) * (1.0 / STEPS))
    steps = ref[0:units].astype(jnp.int32).astype(F32)
    return scale * steps.reshape((2 * units, 8) + ref.shape[2:])


def kernel(clip_bound, context, grad, users, counts, out, held, grad_t, terms, coded_x, coded_y, early_x, early_y,
           same_user, user_count, weight, squares, square_box, norm_box, late_x, late_y, final_x, final_y,
           local_sem, ring_send, ring_recv, side_send, early_send, early_recv, square_send, square_recv,
           norm_send, norm_recv, sum_send, sum_recv, hello):
    data, tensor = lax.axis_index("dp"), lax.axis_index("tensor")
    depth, core = lax.div(tensor, 2), lax.rem(tensor, 2)
    place = (lax.div(data, SIDE), lax.rem(data, SIDE))
    coded, early = (coded_x, coded_y), (early_x, early_y)
    late, final = (late_x, late_y), (final_x, final_y)
    units = (coded_x.shape[3] - 1, coded_y.shape[3] - 1)
    starts = (0, units[0])

    def on_ring(step):
        return lax.rem(depth + step + RING, RING)

    def along(dim, step):
        return lax.rem(place[dim] + step + SIDE, SIDE)

    def at(dim, value):
        return value * SIDE + place[1] if dim == 0 else place[0] * SIDE + value

    right = (data, on_ring(1) * 2 + core)
    left = (data, on_ring(-1) * 2 + core)
    sibling = (data, depth * 2 + 1 - core)
    around = tuple((at(dim, along(dim, step)), tensor) for dim in range(2) for step in (1, -1))

    barrier = pltpu.get_barrier_semaphore()
    for device in (right, left) + around + (sibling,):
        pl.semaphore_signal(barrier, inc=1, device_id=device, device_id_type=MESH)

    load_grad = pltpu.make_async_copy(grad, grad_t, local_sem.at[0])
    loads = []
    for example in range(2):
        for part in range(HALVES):
            loads.append(pltpu.make_async_copy(
                context.at[example, :, pl.ds(part * LANES, LANES)], held.at[tensor, example, part],
                local_sem.at[1 + example * HALVES + part]))
    for copy in loads:
        copy.start()
    load_grad.start()
    for copy in loads:
        copy.wait()

    pl.semaphore_wait(barrier, 7)

    def chunk_copy(slot, example, part, send_sem, device):
        return pltpu.make_async_remote_copy(
            src_ref=held.at[slot, example, part], dst_ref=held.at[slot, example, part], send_sem=send_sem,
            recv_sem=ring_recv.at[slot, example, part], device_id=device, device_id_type=MESH)

    for piece in range(PIECES):
        turn, part = piece // HALVES, piece % HALVES
        chunk_copy(tensor, turn, part, ring_send.at[0, piece], right).start()
        chunk_copy(tensor, 1 - turn, part, ring_send.at[1, piece], left).start()
    for piece in range(PIECES):
        chunk_copy(tensor, piece // HALVES, piece % HALVES, side_send.at[0, piece], sibling).start()

    for turn in range(3):
        for device in around:
            pl.semaphore_signal(hello.at[turn], inc=1, device_id=device, device_id_type=MESH)
        pl.semaphore_wait(hello.at[turn], 4)

    squares[...] = jnp.zeros_like(squares)
    lanes = lax.broadcasted_iota(jnp.int32, (1, LANES), 1)
    everyone = jnp.full((1, LANES), -1, jnp.int32)
    for item in range(2 * GROUP):
        everyone = jnp.where(lanes == item, users[item], everyone)

    @pl.loop(0, 2 * GROUP)
    def _(item):
        same_user[item] = jnp.where(everyone == users[item], 1.0, 0.0)
        user_count[item] = jnp.full((1, LANES), counts[users[item]].astype(F32), F32)

    load_grad.wait()

    def early_copy(dim, slot, example, part):
        spot = (lax.div(slot, SIDE), lax.rem(slot, SIDE))
        return pltpu.make_async_remote_copy(
            src_ref=coded[dim].at[slot, example, part], dst_ref=early[dim].at[place[dim], example, spot[1 - dim], part],
            send_sem=early_send.at[dim], recv_sem=early_recv.at[dim], device_id=(at(dim, spot[dim]), tensor),
            device_id_type=MESH)

    def product(slot, example, part):
        term = jnp.dot(grad_t[example], held[slot, example, part], preferred_element_type=F32)
        tiles = term.reshape(terms.shape[4:])
        spot = (lax.div(slot, SIDE), lax.rem(slot, SIDE))
        terms[example, spot[0], spot[1], part] = tiles
        squares[example] += jnp.sum(tiles * tiles, axis=0)
        steps, powers = encode(tiles)
        for dim in range(2):
            coded[dim][slot, example, part, 0:units[dim]] = steps[starts[dim]:starts[dim] + units[dim]]
            coded[dim][slot, example, part, units[dim]] = powers

            @pl.when(spot[dim] != place[dim])
            def _():
                early_copy(dim, slot, example, part).start()

    def arrived(slot, example, part):
        chunk_copy(slot, example, part, ring_send.at[0, 0], right).wait_recv()

    @pl.loop(0, PIECES)
    def _(piece):
        product(tensor, lax.div(piece, HALVES), lax.rem(piece, HALVES))

    @pl.loop(0, PIECES)
    def _(piece):
        example, part = lax.div(piece, HALVES), lax.rem(piece, HALVES)
        arrived(depth * 2 + 1 - core, example, part)
        product(depth * 2 + 1 - core, example, part)

    @pl.loop(0, STAGES)
    def _(stage):
        distance = 1 + lax.div(stage, PIECES)
        turn = lax.div(lax.rem(stage, PIECES), HALVES)
        part = lax.rem(stage, HALVES)
        sources = ((on_ring(-distance), turn), (on_ring(distance), 1 - turn))
        for way, (source, example) in enumerate(sources):
            slot = source * 2 + core
            arrived(slot, example, part)

            @pl.when(stage < FORWARDS)
            def _():
                chunk_copy(slot, example, part, ring_send.at[way, PIECES + stage], (right, left)[way]).start()

            chunk_copy(slot, example, part, side_send.at[way, PIECES + stage], sibling).start()
        for source, example in sources:
            product(source * 2 + core, example, part)
        for source, example in sources:
            arrived(source * 2 + 1 - core, example, part)
            product(source * 2 + 1 - core, example, part)

    lanes = lax.broadcasted_iota(jnp.int32, (8, LANES), 1)

    def in_lanes(values):
        return jnp.where(lanes == 2 * data, values[0], jnp.where(lanes == 2 * data + 1, values[1], 0.0))

    own = [jnp.sum(jnp.sum(squares[example], axis=0, keepdims=True), axis=1, keepdims=True) for example in range(2)]
    square_box[tensor] = in_lanes(own)

    def square_copy(step, index):
        return pltpu.make_async_remote_copy(
            src_ref=square_box.at[tensor], dst_ref=square_box.at[tensor], send_sem=square_send.at[step],
            recv_sem=square_recv.at[index], device_id=(data, lax.rem(tensor + step, GROUP)), device_id_type=MESH)

    for step in FAR_TENSOR:
        square_copy(step, tensor).start()
    @pl.loop(0, PIECES + STAGES)
    def _(index):
        for way in range(2):
            @pl.when(index < PIECES + FORWARDS)
            def _():
                chunk_copy(0, 0, 0, ring_send.at[way, index], right).wait_send()

            if way == 0:
                chunk_copy(0, 0, 0, side_send.at[way, index], sibling).wait_send()
            else:
                @pl.when(index >= PIECES)
                def _():
                    chunk_copy(0, 0, 0, side_send.at[way, index], sibling).wait_send()

    for step in reversed(FAR_TENSOR):
        square_copy(step, lax.rem(tensor + step, GROUP)).wait_recv()

    norm = jnp.sqrt(jnp.sum(square_box[...], axis=0) + 1e-6)
    norm_box[data] = in_lanes((norm, norm))

    def norm_copy(step, index):
        peer = lax.rem(place[0] + step // SIDE, SIDE) * SIDE + lax.rem(place[1] + step % SIDE, SIDE)
        return pltpu.make_async_remote_copy(
            src_ref=norm_box.at[data], dst_ref=norm_box.at[data], send_sem=norm_send.at[step],
            recv_sem=norm_recv.at[peer if index is None else index], device_id=(peer, tensor), device_id_type=MESH)

    for step in FAR_DATA:
        norm_copy(step, data).start()
    for step in range(1, GROUP):
        square_copy(step, tensor).wait_send()
    for step in reversed(FAR_DATA):
        norm_copy(step, None).wait_recv()

    norms = jnp.sum(norm_box[...], axis=0)[0:1]
    user_norm = jnp.sum(same_user[...] * norms, axis=2, keepdims=True)
    count = user_count[...]
    weight[...] = jnp.minimum(1.0, clip_bound * count / user_norm) / (count * counts.shape[0])

    def all_early(dim):
        whole = early[dim].at[pl.ds(0, SIDE - 1)]
        return pltpu.make_async_remote_copy(
            src_ref=whole, dst_ref=whole, send_sem=early_send.at[dim], recv_sem=early_recv.at[dim],
            device_id=sibling, device_id_type=MESH)

    def gathered(dim, other, part):
        spot = (place[0], other) if dim == 0 else (other, place[1])
        span = pl.ds(2 * starts[dim], 2 * units[dim])
        total = sum(weight[2 * data + example] * terms[(example,) + spot + (part, span)] for example in range(2))
        for step in range(1, SIDE):
            source = along(dim, step)
            for example in range(2):
                total = total + decode(early[dim].at[source, example, other, part], weight[2 * at(dim, source) + example])
        return total

    def sum_copy(dim, step):
        return pltpu.make_async_remote_copy(
            src_ref=late[dim].at[step - 1], dst_ref=final[dim].at[step - 1], send_sem=sum_send.at[dim, step - 1],
            recv_sem=sum_recv.at[dim, step - 1], device_id=(at(1 - dim, along(1 - dim, step)), tensor),
            device_id_type=MESH)

    for dim in range(2):
        all_early(dim).wait_recv()
    for step in (2, 1, 3):
        for dim in range(2):
            for part in range(HALVES):
                steps, powers = encode(gathered(dim, along(1 - dim, step), part))
                late[dim][step - 1, part, 0:units[dim]] = steps
                late[dim][step - 1, part, units[dim]] = powers
            sum_copy(dim, step).start()
    for dim in range(2):
        all_early(dim).wait_send()
    for step in range(1, GROUP):
        norm_copy(step, data).wait_send()
    for dim in range(2):
        for part in range(HALVES):
            span = pl.ds(2 * starts[dim], 2 * units[dim])
            out[span, :, pl.ds(part * LANES, LANES)] = gathered(dim, place[1 - dim], part)
    for step in (1, 3, 2):
        for dim in range(2):
            sum_copy(dim, step).wait_recv()
            for part in range(HALVES):
                span = pl.ds(2 * starts[dim], 2 * units[dim])
                out[span, :, pl.ds(part * LANES, LANES)] += decode(final[dim].at[step - 1, part], 1.0)

    for dim in range(2):
        for step in range(1, SIDE):
            sum_copy(dim, step).wait_send()


def per_device(context, grad, users, counts):
    examples, length, width_in = context.shape
    width_out = grad.shape[2]
    tiles = width_out // 8
    units = (FIRST_UNITS, width_out // 16 - FIRST_UNITS)
    dma = pltpu.SemaphoreType.DMA
    vmem = pltpu.VMEM
    int16 = jnp.int16
    clip_bound = 1.5 * math.sqrt(width_in * width_out * GROUP * GROUP)
    flops = 2 * examples * length * width_in * width_out * GROUP
    result = pl.pallas_call(
        functools.partial(kernel, clip_bound),
        out_shape=vmem((tiles, 8, width_in), F32),
        in_specs=[
            pl.BlockSpec(memory_space=pl.ANY),
            pl.BlockSpec(memory_space=pl.ANY),
            pl.BlockSpec(memory_space=pltpu.SMEM),
            pl.BlockSpec(memory_space=pltpu.SMEM),
        ],
        out_specs=pl.BlockSpec(memory_space=pltpu.VMEM),
        scratch_shapes=[
            vmem((GROUP, examples, HALVES, length, LANES), context.dtype),
            vmem((examples, width_out, length), grad.dtype),
            vmem((examples, SIDE, SIDE, HALVES, tiles, 8, LANES), F32),
            *(vmem((GROUP, examples, HALVES, count + 1, 16, LANES), int16) for count in units),
            *(vmem((SIDE, examples, SIDE, HALVES, count + 1, 16, LANES), int16) for count in units),
            vmem((2 * GROUP, 1, LANES), F32),
            vmem((2 * GROUP, 1, LANES), F32),
            vmem((2 * GROUP, 1, LANES), F32),
            vmem((examples, 8, LANES), F32),
            vmem((GROUP, 8, LANES), F32),
            vmem((GROUP, 8, LANES), F32),
            *(vmem((SIDE - 1, HALVES, count + 1, 16, LANES), int16) for count in units),
            *(vmem((SIDE - 1, HALVES, count + 1, 16, LANES), int16) for count in units),
            dma((1 + PIECES,)),
            dma((2, PIECES + STAGES)),
            dma((GROUP, 2, HALVES)),
            dma((2, PIECES + STAGES)),
            dma((2,)),
            dma((2,)),
            dma((GROUP,)),
            dma((GROUP,)),
            dma((GROUP,)),
            dma((GROUP,)),
            dma((2, SIDE - 1)),
            dma((2, SIDE - 1)),
            pltpu.SemaphoreType.REGULAR((3,)),
        ],
        compiler_params=pltpu.CompilerParams(
            collective_id=0, has_side_effects=True, vmem_limit_bytes=56 * 2**20),
        cost_estimate=pl.CostEstimate(flops=flops, bytes_accessed=2 * context.size + 2 * grad.size, transcendentals=0),
    )(context, jnp.swapaxes(grad, 1, 2), users, counts)
    return result.reshape(width_out, width_in).T


def solution(mesh):
    in_specs = (P("dp", None, "tensor"), P("dp", None, "tensor"), P(), P())
    out_specs = P("dp", "tensor")
    return jax.shard_map(
        per_device, mesh=mesh, in_specs=in_specs, out_specs=out_specs, check_vma=False
    )
```

```python
import functools
import math

import jax
import jax.numpy as jnp
from jax import lax
from jax.experimental import pallas as pl
from jax.experimental.pallas import tpu as pltpu
from jax.sharding import PartitionSpec as P

MESH = pl.DeviceIdType.MESH
F32 = jnp.float32
SIDE = 4
RING = 8
GROUP = 16
LANES = 128
HALVES = 2
PIECES = 2 * HALVES
SIDE_SENDS = 6 * PIECES
STEPS = 32000.0
FAR_TENSOR = sorted(range(1, GROUP), key=lambda step: -min(step, GROUP - step))
FAR_DATA = sorted(range(1, GROUP), key=lambda step: -min(step // SIDE, SIDE - step // SIDE) - min(step % SIDE, SIDE - step % SIDE))


def encode(tiles):
    peak = jnp.max(jnp.max(jnp.abs(tiles), axis=0), axis=0, keepdims=True)
    power = jnp.ceil(jnp.log2(jnp.maximum(peak, 1e-30)))
    steps = jnp.round(tiles * (STEPS * jnp.exp2(-power))[None]).astype(jnp.int32).astype(jnp.int16)
    powers = jnp.broadcast_to(power, (16,) + power.shape[1:]).astype(jnp.int32).astype(jnp.int16)
    return steps.reshape((tiles.shape[0] // 2, 16) + tiles.shape[2:]), powers


def decode(ref, factor):
    units = ref.shape[0] - 1
    power = ref[units].astype(jnp.int32).astype(F32)[0:1]
    scale = factor * (jnp.exp2(power) * (1.0 / STEPS))
    steps = ref[0:units].astype(jnp.int32).astype(F32)
    return scale * steps.reshape((2 * units, 8) + ref.shape[2:])


def kernel(clip_bound, context, grad, users, counts, out, held, grad_own, grad_far, coded, early_x, early_y, late, final,
           same_user, user_count, weight, squares, square_box, norm_box,
           local_sem, ring_recv, far_send, near_send, side_send, grad_send, grad_recv, early_send, early_recv,
           square_send, square_recv, norm_send, norm_recv, total_send, total_recv, hello):
    data, tensor = lax.axis_index("dp"), lax.axis_index("tensor")
    depth, core = lax.div(tensor, 2), lax.rem(tensor, 2)
    place = (lax.div(data, SIDE), lax.rem(data, SIDE))
    units = coded.shape[4] - 1
    early = (early_x, early_y)
    rows = 16 * units
    away = 1 - 2 * lax.rem(depth, 2)

    def plane(step):
        return lax.rem(depth + away * step + RING, RING)

    def along(dim, step):
        return lax.rem(place[dim] + step + SIDE, SIDE)

    def at(dim, value):
        return value * SIDE + place[1] if dim == 0 else place[0] * SIDE + value

    far = (data, plane(1) * 2 + core)
    near = (data, plane(-1) * 2 + core)
    sibling = (data, depth * 2 + 1 - core)
    around = tuple((at(dim, along(dim, step)), tensor) for dim in range(2) for step in (1, -1))

    barrier = pltpu.get_barrier_semaphore()
    for device in (far, near) + around + (sibling,):
        pl.semaphore_signal(barrier, inc=1, device_id=device, device_id_type=MESH)

    loads = []
    for example in range(2):
        for part in range(HALVES):
            number = example * HALVES + part
            loads.append(pltpu.make_async_copy(
                grad.at[example, pl.ds(part * rows, rows)], grad_own.at[example, part], local_sem.at[number]))
            loads.append(pltpu.make_async_copy(
                context.at[example, :, pl.ds(part * LANES, LANES)], held.at[tensor, example, part],
                local_sem.at[PIECES + number]))
    for copy in loads:
        copy.start()
    for copy in loads:
        copy.wait()

    pl.semaphore_wait(barrier, 7)

    def chunk_copy(slot, example, part, send_sem, device):
        return pltpu.make_async_remote_copy(
            src_ref=held.at[slot, example, part], dst_ref=held.at[slot, example, part], send_sem=send_sem,
            recv_sem=ring_recv.at[slot, example, part], device_id=device, device_id_type=MESH)

    def grad_copy(example, part):
        return pltpu.make_async_remote_copy(
            src_ref=grad_own.at[example, part], dst_ref=grad_far.at[example, part],
            send_sem=grad_send.at[example, part], recv_sem=grad_recv.at[example, part],
            device_id=near, device_id_type=MESH)

    for part in range(HALVES):
        grad_copy(0, part).start()
        chunk_copy(tensor, 0, part, far_send.at[part], far).start()
    for piece in range(PIECES):
        example, part = piece // HALVES, piece % HALVES
        chunk_copy(tensor, example, part, near_send.at[piece], near).start()
        if example == 1:
            chunk_copy(tensor, example, part, far_send.at[piece], far).start()
    for piece in range(PIECES):
        chunk_copy(tensor, piece // HALVES, piece % HALVES, side_send.at[piece], sibling).start()

    for turn in range(3):
        for device in around:
            pl.semaphore_signal(hello.at[turn], inc=1, device_id=device, device_id_type=MESH)
        pl.semaphore_wait(hello.at[turn], 4)

    squares[...] = jnp.zeros_like(squares)
    lanes = lax.broadcasted_iota(jnp.int32, (1, LANES), 1)
    everyone = jnp.full((1, LANES), -1, jnp.int32)
    for item in range(2 * GROUP):
        everyone = jnp.where(lanes == item, users[item], everyone)

    @pl.loop(0, 2 * GROUP)
    def _(item):
        same_user[item] = jnp.where(everyone == users[item], 1.0, 0.0)
        user_count[item] = jnp.full((1, LANES), counts[users[item]].astype(F32), F32)

    missing = lax.rem(lax.div(depth, 2) + 2, SIDE)

    def swap(main, other):
        moved = lax.rem(missing + other, SIDE)
        return jnp.where(main == missing, moved, jnp.where(main == moved, missing, main))

    def product(lhs, slot, example, part, tile):
        lhs = lhs.reshape((2 * rows, lhs.shape[2]))
        term = jnp.dot(lhs, held[slot, example, part], preferred_element_type=F32)
        tiles = term.reshape((4 * units, 8, LANES))
        squares[example] += jnp.sum(tiles * tiles, axis=0)
        main, other = lax.div(tile, SIDE), lax.rem(tile, SIDE)
        for half in range(2):
            steps, powers = encode(tiles[2 * units * half:2 * units * (half + 1)])
            coded[tile, example, part, half, 0:units] = steps
            coded[tile, example, part, half, units] = powers
            owner = swap(main, other) if half == 0 else other

            @pl.when(owner != place[half])
            def _():
                pltpu.make_async_remote_copy(
                    src_ref=coded.at[tile, example, part, half],
                    dst_ref=early[half].at[place[half], example, (other, main)[half], part],
                    send_sem=early_send.at[half], recv_sem=early_recv.at[half],
                    device_id=(at(half, owner), tensor), device_id_type=MESH).start()

    def own_product(slot, example, part):
        product(grad_own[example], slot, example, part, slot)

    def far_product(slot, example, part):
        product(grad_far[example], slot, example, part, lax.rem(slot + 4 * away + 2 * RING, 2 * RING))

    def arrived(slot, example, part):
        chunk_copy(slot, example, part, side_send.at[0], sibling).wait_recv()

    def split(piece):
        return lax.div(piece, HALVES), lax.rem(piece, HALVES)

    @pl.loop(0, PIECES)
    def _(piece):
        own_product(tensor, *split(piece))

    @pl.loop(0, PIECES)
    def _(piece):
        arrived(depth * 2 + 1 - core, *split(piece))
        own_product(depth * 2 + 1 - core, *split(piece))

    @pl.loop(0, PIECES)
    def _(piece):
        example, part = split(piece)
        for block, device, send_sem, side in (
                (plane(1), near, near_send.at[PIECES + piece], PIECES), (plane(-1), far, far_send.at[PIECES + piece], 2 * PIECES)):
            slot = block * 2 + core
            arrived(slot, example, part)
            chunk_copy(slot, example, part, send_sem, device).start()
            chunk_copy(slot, example, part, side_send.at[side + piece], sibling).start()
        for block in (plane(1), plane(-1)):
            own_product(block * 2 + core, example, part)
        for block in (plane(1), plane(-1)):
            arrived(block * 2 + 1 - core, example, part)
            own_product(block * 2 + 1 - core, example, part)

    for part in range(HALVES):
        grad_copy(1, part).start()
    for part in range(HALVES):
        grad_copy(0, part).wait_recv()

    @pl.loop(0, PIECES)
    def _(piece):
        example, part = split(piece)
        slot = plane(2) * 2 + core
        arrived(slot, example, part)
        chunk_copy(slot, example, part, side_send.at[3 * PIECES + piece], sibling).start()
        slot = plane(-2) * 2 + core
        arrived(slot, example, part)
        chunk_copy(slot, example, part, far_send.at[2 * PIECES + piece], far).start()
        chunk_copy(slot, example, part, side_send.at[4 * PIECES + piece], sibling).start()
        for block in (plane(2), plane(-2)):
            own_product(block * 2 + core, example, part)
        for block in (plane(2), plane(-2)):
            arrived(block * 2 + 1 - core, example, part)
            own_product(block * 2 + 1 - core, example, part)

        @pl.when(piece < HALVES)
        def _():
            for parity in range(2):
                far_product(plane(2) * 2 + parity, 0, part)

    @pl.loop(0, PIECES)
    def _(piece):
        example, part = split(piece)
        slot = plane(3) * 2 + core
        arrived(slot, example, part)
        chunk_copy(slot, example, part, side_send.at[5 * PIECES + piece], sibling).start()
        own_product(slot, example, part)
        slot = plane(3) * 2 + 1 - core
        arrived(slot, example, part)
        own_product(slot, example, part)

        @pl.when(piece < HALVES)
        def _():
            for parity in range(2):
                far_product(plane(3) * 2 + parity, 0, part)

    for part in range(HALVES):
        grad_copy(1, part).wait_recv()

    @pl.loop(0, 2 * PIECES)
    def _(item):
        block = plane(2 + lax.div(item, PIECES))
        rest = lax.rem(item, PIECES)
        far_product(block * 2 + lax.div(rest, HALVES), 1, lax.rem(rest, HALVES))

    lanes = lax.broadcasted_iota(jnp.int32, (8, LANES), 1)

    def in_lanes(values):
        return jnp.where(lanes == 2 * data, values[0], jnp.where(lanes == 2 * data + 1, values[1], 0.0))

    own = [jnp.sum(jnp.sum(squares[example], axis=0, keepdims=True), axis=1, keepdims=True) for example in range(2)]
    square_box[tensor] = in_lanes(own)

    def square_copy(step, index):
        return pltpu.make_async_remote_copy(
            src_ref=square_box.at[tensor], dst_ref=square_box.at[tensor], send_sem=square_send.at[step],
            recv_sem=square_recv.at[index], device_id=(data, lax.rem(tensor + step, GROUP)), device_id_type=MESH)

    for step in FAR_TENSOR:
        square_copy(step, tensor).start()

    @pl.loop(0, SIDE_SENDS)
    def _(index):
        chunk_copy(0, 0, 0, side_send.at[index], sibling).wait_send()

        @pl.when(index < 3 * PIECES)
        def _():
            chunk_copy(0, 0, 0, far_send.at[index], far).wait_send()

        @pl.when(index < 2 * PIECES)
        def _():
            chunk_copy(0, 0, 0, near_send.at[index], near).wait_send()

    for example in range(2):
        for part in range(HALVES):
            grad_copy(example, part).wait_send()
    for step in reversed(FAR_TENSOR):
        square_copy(step, lax.rem(tensor + step, GROUP)).wait_recv()

    norm = jnp.sqrt(jnp.sum(square_box[...], axis=0) + 1e-6)
    norm_box[data] = in_lanes((norm, norm))

    def norm_copy(step, index):
        peer = lax.rem(place[0] + step // SIDE, SIDE) * SIDE + lax.rem(place[1] + step % SIDE, SIDE)
        return pltpu.make_async_remote_copy(
            src_ref=norm_box.at[data], dst_ref=norm_box.at[data], send_sem=norm_send.at[step],
            recv_sem=norm_recv.at[peer if index is None else index], device_id=(peer, tensor), device_id_type=MESH)

    for step in FAR_DATA:
        norm_copy(step, data).start()
    for step in range(1, GROUP):
        square_copy(step, tensor).wait_send()
    for step in reversed(FAR_DATA):
        norm_copy(step, None).wait_recv()

    norms = jnp.sum(norm_box[...], axis=0)[0:1]
    user_norm = jnp.sum(same_user[...] * norms, axis=2, keepdims=True)
    count = user_count[...]
    weight[...] = jnp.minimum(1.0, clip_bound * count / user_norm) / (count * counts.shape[0])

    def all_early(dim):
        whole = early[dim].at[pl.ds(0, SIDE - 1)]
        return pltpu.make_async_remote_copy(
            src_ref=whole, dst_ref=whole, send_sem=early_send.at[dim], recv_sem=early_recv.at[dim],
            device_id=sibling, device_id_type=MESH)

    def spot(dim, turn):
        if dim == 0:
            other = lax.rem(place[0] - missing + turn + SIDE, SIDE)
            return other, swap(place[0], other), other
        main = lax.rem(missing + turn, SIDE)
        return main, main, place[1]

    def target(dim, turn):
        _, main, other = spot(dim, turn)
        foreign = jnp.where(main == missing, 1, 0)
        row = lax.rem(main * SIDE + other - 4 * away * foreign + GROUP, GROUP)
        return row, plane(-foreign) * 2 + core

    def late_copy(dim, turn):
        return pltpu.make_async_remote_copy(
            src_ref=late.at[dim, turn], dst_ref=final.at[dim, place[1 - dim]], send_sem=total_send.at[dim, turn],
            recv_sem=total_recv.at[dim, place[1 - dim]], device_id=target(dim, turn), device_id_type=MESH)

    def is_here(dim, turn):
        row, column = target(dim, turn)
        return (row == data) & (column == tensor)

    for dim in range(2):
        all_early(dim).wait_recv()
    for turn in range(SIDE):
        for dim in range(2):
            index, main, other = spot(dim, turn)
            for part in range(HALVES):
                total = sum(decode(coded.at[main * SIDE + other, example, part, dim], weight[2 * data + example])
                            for example in range(2))
                for step in range(1, SIDE):
                    source = along(dim, step)
                    for example in range(2):
                        total = total + decode(early[dim].at[source, example, index, part],
                                               weight[2 * at(dim, source) + example])
                steps, powers = encode(total)
                late[dim, turn, part, 0:units] = steps
                late[dim, turn, part, units] = powers

            @pl.when(jnp.logical_not(is_here(dim, turn)))
            def _():
                late_copy(dim, turn).start()

            @pl.when(is_here(dim, turn))
            def _():
                pltpu.make_async_copy(
                    late.at[dim, turn], final.at[dim, place[1 - dim]], total_recv.at[dim, place[1 - dim]]).start()

    for dim in range(2):
        all_early(dim).wait_send()
    for step in range(1, GROUP):
        norm_copy(step, data).wait_send()
    for turn in range(SIDE):
        for dim in range(2):
            @pl.when(jnp.logical_not(is_here(dim, turn)))
            def _():
                late_copy(dim, turn).wait_send()

    for dim in range(2):
        for source in range(SIDE):
            pltpu.make_async_remote_copy(
                src_ref=late.at[0, 0], dst_ref=final.at[dim, source], send_sem=total_send.at[0, 0],
                recv_sem=total_recv.at[dim, source], device_id=sibling, device_id_type=MESH).wait_recv()
        for part in range(HALVES):
            total = sum(decode(final.at[dim, source, part], 1.0) for source in range(SIDE))
            out[pl.ds(2 * units * dim, 2 * units), :, pl.ds(part * LANES, LANES)] = total


def per_device(context, grad, users, counts):
    examples, length, width_in = context.shape
    width_out = grad.shape[2]
    tiles = width_out // 8
    units = width_out // 32
    dma = pltpu.SemaphoreType.DMA
    vmem = pltpu.VMEM
    int16 = jnp.int16
    clip_bound = 1.5 * math.sqrt(width_in * width_out * GROUP * GROUP)
    flops = 2 * examples * length * width_in * width_out * GROUP
    result = pl.pallas_call(
        functools.partial(kernel, clip_bound),
        out_shape=vmem((tiles, 8, width_in), F32),
        in_specs=[
            pl.BlockSpec(memory_space=pl.ANY),
            pl.BlockSpec(memory_space=pl.ANY),
            pl.BlockSpec(memory_space=pltpu.SMEM),
            pl.BlockSpec(memory_space=pltpu.SMEM),
        ],
        out_specs=pl.BlockSpec(memory_space=pltpu.VMEM),
        scratch_shapes=[
            vmem((GROUP, examples, HALVES, length, LANES), context.dtype),
            vmem((examples, HALVES, 16 * units, length), grad.dtype),
            vmem((examples, HALVES, 16 * units, length), grad.dtype),
            vmem((GROUP, examples, HALVES, HALVES, units + 1, 16, LANES), int16),
            vmem((SIDE, examples, SIDE, HALVES, units + 1, 16, LANES), int16),
            vmem((SIDE, examples, SIDE, HALVES, units + 1, 16, LANES), int16),
            vmem((2, SIDE, HALVES, units + 1, 16, LANES), int16),
            vmem((2, SIDE, HALVES, units + 1, 16, LANES), int16),
            vmem((2 * GROUP, 1, LANES), F32),
            vmem((2 * GROUP, 1, LANES), F32),
            vmem((2 * GROUP, 1, LANES), F32),
            vmem((examples, 8, LANES), F32),
            vmem((GROUP, 8, LANES), F32),
            vmem((GROUP, 8, LANES), F32),
            dma((2 * PIECES,)),
            dma((GROUP, 2, HALVES)),
            dma((3 * PIECES,)),
            dma((2 * PIECES,)),
            dma((SIDE_SENDS,)),
            dma((2, HALVES)),
            dma((2, HALVES)),
            dma((2,)),
            dma((2,)),
            dma((GROUP,)),
            dma((GROUP,)),
            dma((GROUP,)),
            dma((GROUP,)),
            dma((2, SIDE)),
            dma((2, SIDE)),
            pltpu.SemaphoreType.REGULAR((3,)),
        ],
        compiler_params=pltpu.CompilerParams(
            collective_id=0, has_side_effects=True, vmem_limit_bytes=56 * 2**20),
        cost_estimate=pl.CostEstimate(flops=flops, bytes_accessed=2 * context.size + 2 * grad.size, transcendentals=0),
    )(context, jnp.swapaxes(grad, 1, 2), users, counts)
    return result.reshape(width_out, width_in).T


def solution(mesh):
    in_specs = (P("dp", None, "tensor"), P("dp", None, "tensor"), P(), P())
    out_specs = P("dp", "tensor")
    return jax.shard_map(
        per_device, mesh=mesh, in_specs=in_specs, out_specs=out_specs, check_vma=False
    )
```

```python
import functools
import math

import jax
import jax.numpy as jnp
from jax import lax
from jax.experimental import pallas as pl
from jax.experimental.pallas import tpu as pltpu
from jax.sharding import PartitionSpec as P

MESH = pl.DeviceIdType.MESH
F32 = jnp.float32
SIDE = 4
RING = 8
GROUP = 16
LANES = 128
HALVES = 2
PIECES = 2 * HALVES
SIDE_SENDS = 6 * PIECES
STEPS = 32000.0
FAR_TENSOR = sorted(range(1, GROUP), key=lambda step: -min(step, GROUP - step))
FAR_DATA = sorted(range(1, GROUP), key=lambda step: -min(step // SIDE, SIDE - step // SIDE) - min(step % SIDE, SIDE - step % SIDE))


def encode(tiles):
    peak = jnp.max(jnp.max(jnp.abs(tiles), axis=0), axis=0, keepdims=True)
    power = jnp.ceil(jnp.log2(jnp.maximum(peak, 1e-30)))
    steps = jnp.round(tiles * (STEPS * jnp.exp2(-power))[None]).astype(jnp.int32).astype(jnp.int16)
    powers = jnp.broadcast_to(power, (16,) + power.shape[1:]).astype(jnp.int32).astype(jnp.int16)
    return steps.reshape((tiles.shape[0] // 2, 16) + tiles.shape[2:]), powers


def decode(ref, factor):
    units = ref.shape[0] - 1
    power = ref[units].astype(jnp.int32).astype(F32)[0:1]
    scale = factor * (jnp.exp2(power) * (1.0 / STEPS))
    steps = ref[0:units].astype(jnp.int32).astype(F32)
    return scale * steps.reshape((2 * units, 8) + ref.shape[2:])


def kernel(clip_bound, context, grad, users, counts, out, held, grad_own, grad_far, coded, early_x, early_y, late, final, spare,
           same_user, user_count, weight, squares, square_box, norm_box,
           local_sem, ring_recv, far_send, near_send, side_send, grad_send, grad_recv, early_send, early_recv,
           square_send, square_recv, norm_send, norm_recv, total_send, total_recv, hello):
    data, tensor = lax.axis_index("dp"), lax.axis_index("tensor")
    depth, core = lax.div(tensor, 2), lax.rem(tensor, 2)
    place = (lax.div(data, SIDE), lax.rem(data, SIDE))
    units = coded.shape[4] - 1
    early = (early_x, early_y)
    rows = 16 * units
    away = 1 - 2 * lax.rem(depth, 2)

    def plane(step):
        return lax.rem(depth + away * step + RING, RING)

    def along(dim, step):
        return lax.rem(place[dim] + step + SIDE, SIDE)

    def at(dim, value):
        return value * SIDE + place[1] if dim == 0 else place[0] * SIDE + value

    far = (data, plane(1) * 2 + core)
    near = (data, plane(-1) * 2 + core)
    sibling = (data, depth * 2 + 1 - core)
    around = tuple((at(dim, along(dim, step)), tensor) for dim in range(2) for step in (1, -1))

    barrier = pltpu.get_barrier_semaphore()
    for device in (far, near) + around + (sibling,):
        pl.semaphore_signal(barrier, inc=1, device_id=device, device_id_type=MESH)

    loads = []
    for example in range(2):
        for part in range(HALVES):
            number = example * HALVES + part
            loads.append(pltpu.make_async_copy(
                grad.at[example, pl.ds(part * rows, rows)], grad_own.at[example, part], local_sem.at[number]))
            loads.append(pltpu.make_async_copy(
                context.at[example, :, pl.ds(part * LANES, LANES)], held.at[tensor, example, part],
                local_sem.at[PIECES + number]))
    for copy in loads:
        copy.start()
    for copy in loads:
        copy.wait()

    pl.semaphore_wait(barrier, 7)

    def chunk_copy(slot, example, part, send_sem, device):
        return pltpu.make_async_remote_copy(
            src_ref=held.at[slot, example, part], dst_ref=held.at[slot, example, part], send_sem=send_sem,
            recv_sem=ring_recv.at[slot, example, part], device_id=device, device_id_type=MESH)

    def grad_copy(example, part):
        return pltpu.make_async_remote_copy(
            src_ref=grad_own.at[example, part], dst_ref=grad_far.at[example, part],
            send_sem=grad_send.at[example, part], recv_sem=grad_recv.at[example, part],
            device_id=near, device_id_type=MESH)

    for part in range(HALVES):
        grad_copy(0, part).start()
        chunk_copy(tensor, 0, part, far_send.at[part], far).start()
    for piece in range(PIECES):
        example, part = piece // HALVES, piece % HALVES
        chunk_copy(tensor, example, part, near_send.at[piece], near).start()
        if example == 1:
            chunk_copy(tensor, example, part, far_send.at[piece], far).start()
    for piece in range(PIECES):
        chunk_copy(tensor, piece // HALVES, piece % HALVES, side_send.at[piece], sibling).start()

    for turn in range(3):
        for device in around:
            pl.semaphore_signal(hello.at[turn], inc=1, device_id=device, device_id_type=MESH)
        pl.semaphore_wait(hello.at[turn], 4)

    squares[...] = jnp.zeros_like(squares)
    lanes = lax.broadcasted_iota(jnp.int32, (1, LANES), 1)
    everyone = jnp.full((1, LANES), -1, jnp.int32)
    for item in range(2 * GROUP):
        everyone = jnp.where(lanes == item, users[item], everyone)

    @pl.loop(0, 2 * GROUP)
    def _(item):
        same_user[item] = jnp.where(everyone == users[item], 1.0, 0.0)
        user_count[item] = jnp.full((1, LANES), counts[users[item]].astype(F32), F32)

    missing = lax.rem(lax.div(depth, 2) + 2, SIDE)

    def swap(main, other):
        moved = lax.rem(missing + other, SIDE)
        return jnp.where(main == missing, moved, jnp.where(main == moved, missing, main))

    def ship(tiles, tile, example, part):
        main, other = lax.div(tile, SIDE), lax.rem(tile, SIDE)
        for half in range(2):
            steps, powers = encode(tiles[2 * units * half:2 * units * (half + 1)])
            coded[tile, example, part, half, 0:units] = steps
            coded[tile, example, part, half, units] = powers
            owner = swap(main, other) if half == 0 else other

            @pl.when(owner != place[half])
            def _():
                pltpu.make_async_remote_copy(
                    src_ref=coded.at[tile, example, part, half],
                    dst_ref=early[half].at[place[half], example, (other, main)[half], part],
                    send_sem=early_send.at[half], recv_sem=early_recv.at[half],
                    device_id=(at(half, owner), tensor), device_id_type=MESH).start()

    def product(lhs, slot, example, part, tile):
        lhs = lhs.reshape((2 * rows, lhs.shape[2]))
        term = jnp.dot(lhs, held[slot, example, part], preferred_element_type=F32)
        tiles = term.reshape((4 * units, 8, LANES))
        squares[example] += jnp.sum(tiles * tiles, axis=0)
        ship(tiles, tile, example, part)

    def own_product(slot, example, part):
        product(grad_own[example], slot, example, part, slot)

    def far_product(slot, example, part):
        product(grad_far[example], slot, example, part, lax.rem(slot + 4 * away + 2 * RING, 2 * RING))

    def arrived(slot, example, part):
        chunk_copy(slot, example, part, side_send.at[0], sibling).wait_recv()

    def split(piece):
        return lax.div(piece, HALVES), lax.rem(piece, HALVES)

    @pl.loop(0, PIECES)
    def _(piece):
        own_product(tensor, *split(piece))

    @pl.loop(0, PIECES)
    def _(piece):
        arrived(depth * 2 + 1 - core, *split(piece))
        own_product(depth * 2 + 1 - core, *split(piece))

    @pl.loop(0, PIECES)
    def _(piece):
        example, part = split(piece)
        for block, device, send_sem, side in (
                (plane(1), near, near_send.at[PIECES + piece], PIECES), (plane(-1), far, far_send.at[PIECES + piece], 2 * PIECES)):
            slot = block * 2 + core
            arrived(slot, example, part)
            chunk_copy(slot, example, part, send_sem, device).start()
            chunk_copy(slot, example, part, side_send.at[side + piece], sibling).start()
        for block in (plane(1), plane(-1)):
            own_product(block * 2 + core, example, part)
        for block in (plane(1), plane(-1)):
            arrived(block * 2 + 1 - core, example, part)
            own_product(block * 2 + 1 - core, example, part)

    for part in range(HALVES):
        grad_copy(1, part).start()
    for part in range(HALVES):
        grad_copy(0, part).wait_recv()

    @pl.loop(0, PIECES)
    def _(piece):
        example, part = split(piece)
        slot = plane(2) * 2 + core
        arrived(slot, example, part)
        chunk_copy(slot, example, part, side_send.at[3 * PIECES + piece], sibling).start()
        slot = plane(-2) * 2 + core
        arrived(slot, example, part)
        chunk_copy(slot, example, part, far_send.at[2 * PIECES + piece], far).start()
        chunk_copy(slot, example, part, side_send.at[4 * PIECES + piece], sibling).start()
        for block in (plane(2), plane(-2)):
            own_product(block * 2 + core, example, part)
        for block in (plane(2), plane(-2)):
            arrived(block * 2 + 1 - core, example, part)
            own_product(block * 2 + 1 - core, example, part)

        @pl.when(piece < HALVES)
        def _():
            for parity in range(2):
                far_product(plane(2) * 2 + parity, 0, part)

    @pl.loop(0, PIECES)
    def _(piece):
        example, part = split(piece)
        slot = plane(3) * 2 + core
        arrived(slot, example, part)
        chunk_copy(slot, example, part, side_send.at[5 * PIECES + piece], sibling).start()
        own_product(slot, example, part)
        slot = plane(3) * 2 + 1 - core
        arrived(slot, example, part)
        own_product(slot, example, part)

        @pl.when(piece < HALVES)
        def _():
            for parity in range(2):
                far_product(plane(3) * 2 + parity, 0, part)

    for part in range(HALVES):
        grad_copy(1, part).wait_recv()

    @pl.loop(0, 4)
    def _(item):
        slot = plane(2 + lax.div(item, 2)) * 2 + lax.rem(item, 2)
        lhs = grad_far[1]
        rhs = jnp.concatenate([held[slot, 1, part] for part in range(HALVES)], axis=1)
        term = jnp.dot(lhs.reshape((2 * rows, lhs.shape[2])), rhs, preferred_element_type=F32)
        tiles = term.reshape((4 * units, 8, HALVES * LANES))
        square = jnp.sum(tiles * tiles, axis=0)
        for part in range(HALVES):
            span = slice(part * LANES, (part + 1) * LANES)
            squares[1] += square[:, span]
            spare[item, part] = tiles[:, :, span]

    lanes = lax.broadcasted_iota(jnp.int32, (8, LANES), 1)

    def in_lanes(values):
        return jnp.where(lanes == 2 * data, values[0], jnp.where(lanes == 2 * data + 1, values[1], 0.0))

    own = [jnp.sum(jnp.sum(squares[example], axis=0, keepdims=True), axis=1, keepdims=True) for example in range(2)]
    square_box[tensor] = in_lanes(own)

    def square_copy(step, index):
        return pltpu.make_async_remote_copy(
            src_ref=square_box.at[tensor], dst_ref=square_box.at[tensor], send_sem=square_send.at[step],
            recv_sem=square_recv.at[index], device_id=(data, lax.rem(tensor + step, GROUP)), device_id_type=MESH)

    for step in FAR_TENSOR:
        square_copy(step, tensor).start()

    @pl.loop(0, 4)
    def _(item):
        tile = lax.rem((plane(2 + lax.div(item, 2)) + 2 * away) * 2 + lax.rem(item, 2) + 2 * RING, 2 * RING)
        for part in range(HALVES):
            ship(spare[item, part], tile, 1, part)

    @pl.loop(0, SIDE_SENDS)
    def _(index):
        chunk_copy(0, 0, 0, side_send.at[index], sibling).wait_send()

        @pl.when(index < 3 * PIECES)
        def _():
            chunk_copy(0, 0, 0, far_send.at[index], far).wait_send()

        @pl.when(index < 2 * PIECES)
        def _():
            chunk_copy(0, 0, 0, near_send.at[index], near).wait_send()

    for example in range(2):
        for part in range(HALVES):
            grad_copy(example, part).wait_send()
    for step in reversed(FAR_TENSOR):
        square_copy(step, lax.rem(tensor + step, GROUP)).wait_recv()

    norm = jnp.sqrt(jnp.sum(square_box[...], axis=0) + 1e-6)
    norm_box[data] = in_lanes((norm, norm))

    def norm_copy(step, index):
        peer = lax.rem(place[0] + step // SIDE, SIDE) * SIDE + lax.rem(place[1] + step % SIDE, SIDE)
        return pltpu.make_async_remote_copy(
            src_ref=norm_box.at[data], dst_ref=norm_box.at[data], send_sem=norm_send.at[step],
            recv_sem=norm_recv.at[peer if index is None else index], device_id=(peer, tensor), device_id_type=MESH)

    for step in FAR_DATA:
        norm_copy(step, data).start()
    for step in range(1, GROUP):
        square_copy(step, tensor).wait_send()
    for step in reversed(FAR_DATA):
        norm_copy(step, None).wait_recv()

    norms = jnp.sum(norm_box[...], axis=0)[0:1]
    user_norm = jnp.sum(same_user[...] * norms, axis=2, keepdims=True)
    count = user_count[...]
    weight[...] = jnp.minimum(1.0, clip_bound * count / user_norm) / (count * counts.shape[0])

    def all_early(dim):
        whole = early[dim].at[pl.ds(0, SIDE - 1)]
        return pltpu.make_async_remote_copy(
            src_ref=whole, dst_ref=whole, send_sem=early_send.at[dim], recv_sem=early_recv.at[dim],
            device_id=sibling, device_id_type=MESH)

    def spot(dim, turn):
        first = lax.rem((place[0] - missing if dim == 0 else missing) - place[1 - dim] * (1 - dim) - place[0] * dim + 2 * SIDE, SIDE)
        step = (first, jnp.where(first == 2, 1, 2), jnp.where((first == 1) | (first == 2), 3, 1),
                jnp.where(first == 0, 3, 0))[turn]
        if dim == 0:
            other = lax.rem(place[1] + step, SIDE)
            return other, swap(place[0], other), other
        main = lax.rem(place[0] + step, SIDE)
        return main, main, place[1]

    def target(dim, turn):
        _, main, other = spot(dim, turn)
        foreign = jnp.where(main == missing, 1, 0)
        row = lax.rem(main * SIDE + other - 4 * away * foreign + GROUP, GROUP)
        return row, plane(-foreign) * 2 + core

    def late_copy(dim, turn):
        return pltpu.make_async_remote_copy(
            src_ref=late.at[dim, turn], dst_ref=final.at[dim, place[1 - dim]], send_sem=total_send.at[dim, turn],
            recv_sem=total_recv.at[dim, place[1 - dim]], device_id=target(dim, turn), device_id_type=MESH)

    def is_here(dim, turn):
        row, column = target(dim, turn)
        return (row == data) & (column == tensor)

    for dim in range(2):
        all_early(dim).wait_recv()
    for turn in range(SIDE):
        for dim in range(2):
            index, main, other = spot(dim, turn)
            for part in range(HALVES):
                total = sum(decode(coded.at[main * SIDE + other, example, part, dim], weight[2 * data + example])
                            for example in range(2))
                for step in range(1, SIDE):
                    source = along(dim, step)
                    for example in range(2):
                        total = total + decode(early[dim].at[source, example, index, part],
                                               weight[2 * at(dim, source) + example])
                steps, powers = encode(total)
                late[dim, turn, part, 0:units] = steps
                late[dim, turn, part, units] = powers

            @pl.when(jnp.logical_not(is_here(dim, turn)))
            def _():
                late_copy(dim, turn).start()

            @pl.when(is_here(dim, turn))
            def _():
                pltpu.make_async_copy(
                    late.at[dim, turn], final.at[dim, place[1 - dim]], total_recv.at[dim, place[1 - dim]]).start()

    for dim in range(2):
        all_early(dim).wait_send()
    for step in range(1, GROUP):
        norm_copy(step, data).wait_send()
    for turn in range(SIDE):
        for dim in range(2):
            @pl.when(jnp.logical_not(is_here(dim, turn)))
            def _():
                late_copy(dim, turn).wait_send()

    for dim in range(2):
        for source in range(SIDE):
            pltpu.make_async_remote_copy(
                src_ref=late.at[0, 0], dst_ref=final.at[dim, source], send_sem=total_send.at[0, 0],
                recv_sem=total_recv.at[dim, source], device_id=sibling, device_id_type=MESH).wait_recv()
        for part in range(HALVES):
            total = sum(decode(final.at[dim, source, part], 1.0) for source in range(SIDE))
            out[pl.ds(2 * units * dim, 2 * units), :, pl.ds(part * LANES, LANES)] = total


def per_device(context, grad, users, counts):
    examples, length, width_in = context.shape
    width_out = grad.shape[2]
    tiles = width_out // 8
    units = width_out // 32
    dma = pltpu.SemaphoreType.DMA
    vmem = pltpu.VMEM
    int16 = jnp.int16
    clip_bound = 1.5 * math.sqrt(width_in * width_out * GROUP * GROUP)
    flops = 2 * examples * length * width_in * width_out * GROUP
    result = pl.pallas_call(
        functools.partial(kernel, clip_bound),
        out_shape=vmem((tiles, 8, width_in), F32),
        in_specs=[
            pl.BlockSpec(memory_space=pl.ANY),
            pl.BlockSpec(memory_space=pl.ANY),
            pl.BlockSpec(memory_space=pltpu.SMEM),
            pl.BlockSpec(memory_space=pltpu.SMEM),
        ],
        out_specs=pl.BlockSpec(memory_space=pltpu.VMEM),
        scratch_shapes=[
            vmem((GROUP, examples, HALVES, length, LANES), context.dtype),
            vmem((examples, HALVES, 16 * units, length), grad.dtype),
            vmem((examples, HALVES, 16 * units, length), grad.dtype),
            vmem((GROUP, examples, HALVES, HALVES, units + 1, 16, LANES), int16),
            vmem((SIDE, examples, SIDE, HALVES, units + 1, 16, LANES), int16),
            vmem((SIDE, examples, SIDE, HALVES, units + 1, 16, LANES), int16),
            vmem((2, SIDE, HALVES, units + 1, 16, LANES), int16),
            vmem((2, SIDE, HALVES, units + 1, 16, LANES), int16),
            vmem((4, HALVES, tiles, 8, LANES), F32),
            vmem((2 * GROUP, 1, LANES), F32),
            vmem((2 * GROUP, 1, LANES), F32),
            vmem((2 * GROUP, 1, LANES), F32),
            vmem((examples, 8, LANES), F32),
            vmem((GROUP, 8, LANES), F32),
            vmem((GROUP, 8, LANES), F32),
            dma((2 * PIECES,)),
            dma((GROUP, 2, HALVES)),
            dma((3 * PIECES,)),
            dma((2 * PIECES,)),
            dma((SIDE_SENDS,)),
            dma((2, HALVES)),
            dma((2, HALVES)),
            dma((2,)),
            dma((2,)),
            dma((GROUP,)),
            dma((GROUP,)),
            dma((GROUP,)),
            dma((GROUP,)),
            dma((2, SIDE)),
            dma((2, SIDE)),
            pltpu.SemaphoreType.REGULAR((3,)),
        ],
        compiler_params=pltpu.CompilerParams(
            collective_id=0, has_side_effects=True, vmem_limit_bytes=56 * 2**20),
        cost_estimate=pl.CostEstimate(flops=flops, bytes_accessed=2 * context.size + 2 * grad.size, transcendentals=0),
    )(context, jnp.swapaxes(grad, 1, 2), users, counts)
    return result.reshape(width_out, width_in).T


def solution(mesh):
    in_specs = (P("dp", None, "tensor"), P("dp", None, "tensor"), P(), P())
    out_specs = P("dp", "tensor")
    return jax.shard_map(
        per_device, mesh=mesh, in_specs=in_specs, out_specs=out_specs, check_vma=False
    )
```

```python
import functools
import math

import jax
import jax.numpy as jnp
from jax import lax
from jax.experimental import pallas as pl
from jax.experimental.pallas import tpu as pltpu
from jax.sharding import PartitionSpec as P

MESH = pl.DeviceIdType.MESH
F32 = jnp.float32
SIDE = 4
RING = 8
GROUP = 16
LANES = 128
HALVES = 2
PIECES = 2 * HALVES
SIDE_SENDS = 6 * PIECES
STEPS = 32000.0
FAR_TENSOR = sorted(range(1, GROUP), key=lambda step: -min(step, GROUP - step))
FAR_DATA = sorted(range(1, GROUP), key=lambda step: -min(step // SIDE, SIDE - step // SIDE) - min(step % SIDE, SIDE - step % SIDE))


def encode(tiles):
    peak = jnp.max(jnp.max(jnp.abs(tiles), axis=0), axis=0, keepdims=True)
    power = jnp.ceil(jnp.log2(jnp.maximum(peak, 1e-30)))
    steps = jnp.round(tiles * (STEPS * jnp.exp2(-power))[None]).astype(jnp.int32).astype(jnp.int16)
    powers = jnp.broadcast_to(power, (16,) + power.shape[1:]).astype(jnp.int32).astype(jnp.int16)
    return steps.reshape((tiles.shape[0] // 2, 16) + tiles.shape[2:]), powers


def decode(ref, factor):
    units = ref.shape[0] - 1
    power = ref[units].astype(jnp.int32).astype(F32)[0:1]
    scale = factor * (jnp.exp2(power) * (1.0 / STEPS))
    steps = ref[0:units].astype(jnp.int32).astype(F32)
    return scale * steps.reshape((2 * units, 8) + ref.shape[2:])


def kernel(clip_bound, context, grad, users, counts, out, held, grad_own, grad_far, coded, early_x, early_y, late, final, spare,
           same_user, user_count, weight, squares, square_box, norm_box,
           local_sem, ring_recv, far_send, near_send, side_send, grad_send, grad_recv, early_send, early_recv,
           square_send, square_recv, norm_send, norm_recv, total_send, total_recv, hello):
    data, tensor = lax.axis_index("dp"), lax.axis_index("tensor")
    depth, core = lax.div(tensor, 2), lax.rem(tensor, 2)
    place = (lax.div(data, SIDE), lax.rem(data, SIDE))
    units = coded.shape[4] - 1
    early = (early_x, early_y)
    rows = 16 * units
    away = 1 - 2 * lax.rem(depth, 2)

    def plane(step):
        return lax.rem(depth + away * step + RING, RING)

    def along(dim, step):
        return lax.rem(place[dim] + step + SIDE, SIDE)

    def at(dim, value):
        return value * SIDE + place[1] if dim == 0 else place[0] * SIDE + value

    far = (data, plane(1) * 2 + core)
    near = (data, plane(-1) * 2 + core)
    sibling = (data, depth * 2 + 1 - core)
    around = tuple((at(dim, along(dim, step)), tensor) for dim in range(2) for step in (1, -1))

    barrier = pltpu.get_barrier_semaphore()
    for device in (far, near) + around + (sibling,):
        pl.semaphore_signal(barrier, inc=1, device_id=device, device_id_type=MESH)

    loads = []
    for example in range(2):
        for part in range(HALVES):
            number = example * HALVES + part
            loads.append(pltpu.make_async_copy(
                grad.at[example, pl.ds(part * rows, rows)], grad_own.at[example, part], local_sem.at[number]))
            loads.append(pltpu.make_async_copy(
                context.at[example, :, pl.ds(part * LANES, LANES)], held.at[tensor, example, part],
                local_sem.at[PIECES + number]))
    for copy in loads:
        copy.start()

    pl.semaphore_wait(barrier, 7)

    def chunk_copy(slot, example, part, send_sem, device):
        return pltpu.make_async_remote_copy(
            src_ref=held.at[slot, example, part], dst_ref=held.at[slot, example, part], send_sem=send_sem,
            recv_sem=ring_recv.at[slot, example, part], device_id=device, device_id_type=MESH)

    def own_copy(example, part, send_sem, device):
        return pltpu.make_async_remote_copy(
            src_ref=context.at[example, :, pl.ds(part * LANES, LANES)], dst_ref=held.at[tensor, example, part],
            send_sem=send_sem, recv_sem=ring_recv.at[tensor, example, part], device_id=device, device_id_type=MESH)

    def grad_copy(example, part):
        return pltpu.make_async_remote_copy(
            src_ref=grad.at[example, pl.ds(part * rows, rows)], dst_ref=grad_far.at[example, part],
            send_sem=grad_send.at[example, part], recv_sem=grad_recv.at[example, part],
            device_id=near, device_id_type=MESH)

    for part in range(HALVES):
        grad_copy(0, part).start()
        own_copy(0, part, far_send.at[part], far).start()
    for piece in range(PIECES):
        example, part = piece // HALVES, piece % HALVES
        own_copy(example, part, near_send.at[piece], near).start()
        if example == 1:
            own_copy(example, part, far_send.at[piece], far).start()
    for piece in range(PIECES):
        own_copy(piece // HALVES, piece % HALVES, side_send.at[piece], sibling).start()

    for turn in range(3):
        for device in around:
            pl.semaphore_signal(hello.at[turn], inc=1, device_id=device, device_id_type=MESH)
        pl.semaphore_wait(hello.at[turn], 4)

    squares[...] = jnp.zeros_like(squares)
    lanes = lax.broadcasted_iota(jnp.int32, (1, LANES), 1)
    everyone = jnp.full((1, LANES), -1, jnp.int32)
    for item in range(2 * GROUP):
        everyone = jnp.where(lanes == item, users[item], everyone)

    @pl.loop(0, 2 * GROUP)
    def _(item):
        same_user[item] = jnp.where(everyone == users[item], 1.0, 0.0)
        user_count[item] = jnp.full((1, LANES), counts[users[item]].astype(F32), F32)

    missing = lax.rem(lax.div(depth, 2) + 2, SIDE)

    def swap(main, other):
        moved = lax.rem(missing + other, SIDE)
        return jnp.where(main == missing, moved, jnp.where(main == moved, missing, main))

    def ship(tiles, tile, example, part):
        main, other = lax.div(tile, SIDE), lax.rem(tile, SIDE)
        for half in range(2):
            steps, powers = encode(tiles[2 * units * half:2 * units * (half + 1)])
            coded[tile, example, part, half, 0:units] = steps
            coded[tile, example, part, half, units] = powers
            owner = swap(main, other) if half == 0 else other

            @pl.when(owner != place[half])
            def _():
                pltpu.make_async_remote_copy(
                    src_ref=coded.at[tile, example, part, half],
                    dst_ref=early[half].at[place[half], example, (other, main)[half], part],
                    send_sem=early_send.at[half], recv_sem=early_recv.at[half],
                    device_id=(at(half, owner), tensor), device_id_type=MESH).start()

    def product(lhs, slot, example, part, tile):
        lhs = lhs.reshape((2 * rows, lhs.shape[2]))
        term = jnp.dot(lhs, held[slot, example, part], preferred_element_type=F32)
        tiles = term.reshape((4 * units, 8, LANES))
        squares[example] += jnp.sum(tiles * tiles, axis=0)
        ship(tiles, tile, example, part)

    def own_product(slot, example, part):
        product(grad_own[example], slot, example, part, slot)

    def far_product(slot, example, part):
        product(grad_far[example], slot, example, part, lax.rem(slot + 4 * away + 2 * RING, 2 * RING))

    def arrived(slot, example, part):
        chunk_copy(slot, example, part, side_send.at[0], sibling).wait_recv()

    def split(piece):
        return lax.div(piece, HALVES), lax.rem(piece, HALVES)

    for copy in loads:
        copy.wait()

    @pl.loop(0, PIECES)
    def _(piece):
        own_product(tensor, *split(piece))

    @pl.loop(0, PIECES)
    def _(piece):
        arrived(depth * 2 + 1 - core, *split(piece))
        own_product(depth * 2 + 1 - core, *split(piece))

    @pl.loop(0, PIECES)
    def _(piece):
        example, part = split(piece)
        for block, device, send_sem, side in (
                (plane(1), near, near_send.at[PIECES + piece], PIECES), (plane(-1), far, far_send.at[PIECES + piece], 2 * PIECES)):
            slot = block * 2 + core
            arrived(slot, example, part)
            chunk_copy(slot, example, part, send_sem, device).start()
            chunk_copy(slot, example, part, side_send.at[side + piece], sibling).start()
        for block in (plane(1), plane(-1)):
            own_product(block * 2 + core, example, part)
        for block in (plane(1), plane(-1)):
            arrived(block * 2 + 1 - core, example, part)
            own_product(block * 2 + 1 - core, example, part)

    for part in range(HALVES):
        grad_copy(1, part).start()
    for part in range(HALVES):
        grad_copy(0, part).wait_recv()

    @pl.loop(0, PIECES)
    def _(piece):
        example, part = split(piece)
        slot = plane(2) * 2 + core
        arrived(slot, example, part)
        chunk_copy(slot, example, part, side_send.at[3 * PIECES + piece], sibling).start()
        slot = plane(-2) * 2 + core
        arrived(slot, example, part)
        chunk_copy(slot, example, part, far_send.at[2 * PIECES + piece], far).start()
        chunk_copy(slot, example, part, side_send.at[4 * PIECES + piece], sibling).start()
        for block in (plane(2), plane(-2)):
            own_product(block * 2 + core, example, part)
        for block in (plane(2), plane(-2)):
            arrived(block * 2 + 1 - core, example, part)
            own_product(block * 2 + 1 - core, example, part)

        @pl.when(piece < HALVES)
        def _():
            for parity in range(2):
                far_product(plane(2) * 2 + parity, 0, part)

    @pl.loop(0, PIECES)
    def _(piece):
        example, part = split(piece)
        slot = plane(3) * 2 + core
        arrived(slot, example, part)
        chunk_copy(slot, example, part, side_send.at[5 * PIECES + piece], sibling).start()
        own_product(slot, example, part)
        slot = plane(3) * 2 + 1 - core
        arrived(slot, example, part)
        own_product(slot, example, part)

        @pl.when(piece < HALVES)
        def _():
            for parity in range(2):
                far_product(plane(3) * 2 + parity, 0, part)

    for part in range(HALVES):
        grad_copy(1, part).wait_recv()

    @pl.loop(0, 4)
    def _(item):
        slot = plane(2 + lax.div(item, 2)) * 2 + lax.rem(item, 2)
        lhs = grad_far[1]
        rhs = jnp.concatenate([held[slot, 1, part] for part in range(HALVES)], axis=1)
        term = jnp.dot(lhs.reshape((2 * rows, lhs.shape[2])), rhs, preferred_element_type=F32)
        tiles = term.reshape((4 * units, 8, HALVES * LANES))
        square = jnp.sum(tiles * tiles, axis=0)
        for part in range(HALVES):
            span = slice(part * LANES, (part + 1) * LANES)
            squares[1] += square[:, span]
            spare[item, part] = tiles[:, :, span]

    lanes = lax.broadcasted_iota(jnp.int32, (8, LANES), 1)

    def in_lanes(values):
        return jnp.where(lanes == 2 * data, values[0], jnp.where(lanes == 2 * data + 1, values[1], 0.0))

    own = [jnp.sum(jnp.sum(squares[example], axis=0, keepdims=True), axis=1, keepdims=True) for example in range(2)]
    square_box[tensor] = in_lanes(own)

    def square_copy(step, index):
        return pltpu.make_async_remote_copy(
            src_ref=square_box.at[tensor], dst_ref=square_box.at[tensor], send_sem=square_send.at[step],
            recv_sem=square_recv.at[index], device_id=(data, lax.rem(tensor + step, GROUP)), device_id_type=MESH)

    for step in FAR_TENSOR:
        square_copy(step, tensor).start()

    @pl.loop(0, 4)
    def _(item):
        tile = lax.rem((plane(2 + lax.div(item, 2)) + 2 * away) * 2 + lax.rem(item, 2) + 2 * RING, 2 * RING)
        for part in range(HALVES):
            ship(spare[item, part], tile, 1, part)

    @pl.loop(0, SIDE_SENDS)
    def _(index):
        chunk_copy(0, 0, 0, side_send.at[index], sibling).wait_send()

        @pl.when(index < 3 * PIECES)
        def _():
            chunk_copy(0, 0, 0, far_send.at[index], far).wait_send()

        @pl.when(index < 2 * PIECES)
        def _():
            chunk_copy(0, 0, 0, near_send.at[index], near).wait_send()

    for example in range(2):
        for part in range(HALVES):
            grad_copy(example, part).wait_send()
    for step in reversed(FAR_TENSOR):
        square_copy(step, lax.rem(tensor + step, GROUP)).wait_recv()

    norm = jnp.sqrt(jnp.sum(square_box[...], axis=0) + 1e-6)
    norm_box[data] = in_lanes((norm, norm))

    def norm_copy(step, index):
        peer = lax.rem(place[0] + step // SIDE, SIDE) * SIDE + lax.rem(place[1] + step % SIDE, SIDE)
        return pltpu.make_async_remote_copy(
            src_ref=norm_box.at[data], dst_ref=norm_box.at[data], send_sem=norm_send.at[step],
            recv_sem=norm_recv.at[peer if index is None else index], device_id=(peer, tensor), device_id_type=MESH)

    for step in FAR_DATA:
        norm_copy(step, data).start()
    for step in range(1, GROUP):
        square_copy(step, tensor).wait_send()
    for step in reversed(FAR_DATA):
        norm_copy(step, None).wait_recv()

    norms = jnp.sum(norm_box[...], axis=0)[0:1]
    user_norm = jnp.sum(same_user[...] * norms, axis=2, keepdims=True)
    count = user_count[...]
    weight[...] = jnp.minimum(1.0, clip_bound * count / user_norm) / (count * counts.shape[0])

    def all_early(dim):
        whole = early[dim].at[pl.ds(0, SIDE - 1)]
        return pltpu.make_async_remote_copy(
            src_ref=whole, dst_ref=whole, send_sem=early_send.at[dim], recv_sem=early_recv.at[dim],
            device_id=sibling, device_id_type=MESH)

    def spot(dim, turn):
        first = lax.rem((place[0] - missing if dim == 0 else missing) - place[1 - dim] * (1 - dim) - place[0] * dim + 2 * SIDE, SIDE)
        order = (first, jnp.where(first == 2, 1, 2), jnp.where((first == 1) | (first == 2), 3, 1),
                 jnp.where(first == 0, 3, 0))
        swapped = (order[0], order[2], order[1], order[3])
        step = jnp.where(core == dim, order[turn], swapped[turn])
        if dim == 0:
            other = lax.rem(place[1] + step, SIDE)
            return other, swap(place[0], other), other
        main = lax.rem(place[0] + step, SIDE)
        return main, main, place[1]

    def target(dim, turn):
        _, main, other = spot(dim, turn)
        foreign = jnp.where(main == missing, 1, 0)
        row = lax.rem(main * SIDE + other - 4 * away * foreign + GROUP, GROUP)
        return row, plane(-foreign) * 2 + core

    def late_copy(dim, turn):
        return pltpu.make_async_remote_copy(
            src_ref=late.at[dim, turn], dst_ref=final.at[dim, place[1 - dim]], send_sem=total_send.at[dim, turn],
            recv_sem=total_recv.at[dim, place[1 - dim]], device_id=target(dim, turn), device_id_type=MESH)

    def is_here(dim, turn):
        row, column = target(dim, turn)
        return (row == data) & (column == tensor)

    for dim in range(2):
        all_early(dim).wait_recv()
    for turn in range(SIDE):
        for dim in range(2):
            index, main, other = spot(dim, turn)
            for part in range(HALVES):
                total = sum(decode(coded.at[main * SIDE + other, example, part, dim], weight[2 * data + example])
                            for example in range(2))
                for step in range(1, SIDE):
                    source = along(dim, step)
                    for example in range(2):
                        total = total + decode(early[dim].at[source, example, index, part],
                                               weight[2 * at(dim, source) + example])
                steps, powers = encode(total)
                late[dim, turn, part, 0:units] = steps
                late[dim, turn, part, units] = powers

            @pl.when(jnp.logical_not(is_here(dim, turn)))
            def _():
                late_copy(dim, turn).start()

            @pl.when(is_here(dim, turn))
            def _():
                pltpu.make_async_copy(
                    late.at[dim, turn], final.at[dim, place[1 - dim]], total_recv.at[dim, place[1 - dim]]).start()

    for dim in range(2):
        all_early(dim).wait_send()
    for step in range(1, GROUP):
        norm_copy(step, data).wait_send()
    for turn in range(SIDE):
        for dim in range(2):
            @pl.when(jnp.logical_not(is_here(dim, turn)))
            def _():
                late_copy(dim, turn).wait_send()

    for dim in range(2):
        for source in range(SIDE):
            pltpu.make_async_remote_copy(
                src_ref=late.at[0, 0], dst_ref=final.at[dim, source], send_sem=total_send.at[0, 0],
                recv_sem=total_recv.at[dim, source], device_id=sibling, device_id_type=MESH).wait_recv()
        for part in range(HALVES):
            total = sum(decode(final.at[dim, source, part], 1.0) for source in range(SIDE))
            out[pl.ds(2 * units * dim, 2 * units), :, pl.ds(part * LANES, LANES)] = total


def per_device(context, grad, users, counts):
    examples, length, width_in = context.shape
    width_out = grad.shape[2]
    tiles = width_out // 8
    units = width_out // 32
    dma = pltpu.SemaphoreType.DMA
    vmem = pltpu.VMEM
    int16 = jnp.int16
    clip_bound = 1.5 * math.sqrt(width_in * width_out * GROUP * GROUP)
    flops = 2 * examples * length * width_in * width_out * GROUP
    result = pl.pallas_call(
        functools.partial(kernel, clip_bound),
        out_shape=vmem((tiles, 8, width_in), F32),
        in_specs=[
            pl.BlockSpec(memory_space=pl.ANY),
            pl.BlockSpec(memory_space=pl.ANY),
            pl.BlockSpec(memory_space=pltpu.SMEM),
            pl.BlockSpec(memory_space=pltpu.SMEM),
        ],
        out_specs=pl.BlockSpec(memory_space=pltpu.VMEM),
        scratch_shapes=[
            vmem((GROUP, examples, HALVES, length, LANES), context.dtype),
            vmem((examples, HALVES, 16 * units, length), grad.dtype),
            vmem((examples, HALVES, 16 * units, length), grad.dtype),
            vmem((GROUP, examples, HALVES, HALVES, units + 1, 16, LANES), int16),
            vmem((SIDE, examples, SIDE, HALVES, units + 1, 16, LANES), int16),
            vmem((SIDE, examples, SIDE, HALVES, units + 1, 16, LANES), int16),
            vmem((2, SIDE, HALVES, units + 1, 16, LANES), int16),
            vmem((2, SIDE, HALVES, units + 1, 16, LANES), int16),
            vmem((4, HALVES, tiles, 8, LANES), F32),
            vmem((2 * GROUP, 1, LANES), F32),
            vmem((2 * GROUP, 1, LANES), F32),
            vmem((2 * GROUP, 1, LANES), F32),
            vmem((examples, 8, LANES), F32),
            vmem((GROUP, 8, LANES), F32),
            vmem((GROUP, 8, LANES), F32),
            dma((2 * PIECES,)),
            dma((GROUP, 2, HALVES)),
            dma((3 * PIECES,)),
            dma((2 * PIECES,)),
            dma((SIDE_SENDS,)),
            dma((2, HALVES)),
            dma((2, HALVES)),
            dma((2,)),
            dma((2,)),
            dma((GROUP,)),
            dma((GROUP,)),
            dma((GROUP,)),
            dma((GROUP,)),
            dma((2, SIDE)),
            dma((2, SIDE)),
            pltpu.SemaphoreType.REGULAR((3,)),
        ],
        compiler_params=pltpu.CompilerParams(
            collective_id=0, has_side_effects=True, vmem_limit_bytes=56 * 2**20),
        cost_estimate=pl.CostEstimate(flops=flops, bytes_accessed=2 * context.size + 2 * grad.size, transcendentals=0),
    )(context, jnp.swapaxes(grad, 1, 2), users, counts)
    return result.reshape(width_out, width_in).T


def solution(mesh):
    in_specs = (P("dp", None, "tensor"), P("dp", None, "tensor"), P(), P())
    out_specs = P("dp", "tensor")
    return jax.shard_map(
        per_device, mesh=mesh, in_specs=in_specs, out_specs=out_specs, check_vma=False
    )
```

```python
import functools
import math

import jax
import jax.numpy as jnp
from jax import lax
from jax.experimental import pallas as pl
from jax.experimental.pallas import tpu as pltpu
from jax.sharding import PartitionSpec as P

MESH = pl.DeviceIdType.MESH
F32 = jnp.float32
SIDE = 4
RING = 8
GROUP = 16
LANES = 128
HALVES = 2
PIECES = 2 * HALVES
SIDE_SENDS = 6 * PIECES
STEPS = 32000.0
FAR_TENSOR = sorted(range(1, GROUP), key=lambda step: -min(step, GROUP - step))
FAR_DATA = sorted(range(1, GROUP), key=lambda step: -min(step // SIDE, SIDE - step // SIDE) - min(step % SIDE, SIDE - step % SIDE))


def encode(tiles):
    peak = jnp.max(jnp.max(jnp.abs(tiles), axis=0), axis=0, keepdims=True)
    power = jnp.ceil(jnp.log2(jnp.maximum(peak, 1e-30)))
    steps = jnp.round(tiles * (STEPS * jnp.exp2(-power))[None]).astype(jnp.int32).astype(jnp.int16)
    powers = jnp.broadcast_to(power, (16,) + power.shape[1:]).astype(jnp.int32).astype(jnp.int16)
    return steps.reshape((tiles.shape[0] // 2, 16) + tiles.shape[2:]), powers


def decode(ref, factor):
    units = ref.shape[0] - 1
    power = ref[units].astype(jnp.int32).astype(F32)[0:1]
    scale = factor * (jnp.exp2(power) * (1.0 / STEPS))
    steps = ref[0:units].astype(jnp.int32).astype(F32)
    return scale * steps.reshape((2 * units, 8) + ref.shape[2:])


def landed(ref, part):
    units = ref.shape[0] // 2
    power = ref[2 * units].astype(jnp.int32).astype(F32)[8 * part:8 * part + 1]
    steps = ref[part * units:(part + 1) * units].astype(jnp.int32).astype(F32)
    return (jnp.exp2(power) * (1.0 / STEPS)) * steps.reshape((2 * units, 8) + ref.shape[2:])


def kernel(clip_bound, context, grad, users, counts, out, held, grad_own, grad_far, coded, early_x, early_y, late, final, spare,
           same_user, user_count, weight, squares, square_box, norm_box,
           local_sem, ring_recv, far_send, near_send, side_send, grad_send, grad_recv, early_send, early_recv,
           square_send, square_recv, norm_send, norm_recv, total_send, total_recv, hello):
    data, tensor = lax.axis_index("dp"), lax.axis_index("tensor")
    depth, core = lax.div(tensor, 2), lax.rem(tensor, 2)
    place = (lax.div(data, SIDE), lax.rem(data, SIDE))
    units = coded.shape[4] - 1
    early = (early_x, early_y)
    rows = 16 * units
    away = 1 - 2 * lax.rem(depth, 2)

    def plane(step):
        return lax.rem(depth + away * step + RING, RING)

    def along(dim, step):
        return lax.rem(place[dim] + step + SIDE, SIDE)

    def at(dim, value):
        return value * SIDE + place[1] if dim == 0 else place[0] * SIDE + value

    far = (data, plane(1) * 2 + core)
    near = (data, plane(-1) * 2 + core)
    sibling = (data, depth * 2 + 1 - core)
    around = tuple((at(dim, along(dim, step)), tensor) for dim in range(2) for step in (1, -1))

    barrier = pltpu.get_barrier_semaphore()
    for device in (far, near) + around + (sibling,):
        pl.semaphore_signal(barrier, inc=1, device_id=device, device_id_type=MESH)

    loads = []
    for example in range(2):
        for part in range(HALVES):
            number = example * HALVES + part
            loads.append(pltpu.make_async_copy(
                grad.at[example, pl.ds(part * rows, rows)], grad_own.at[example, part], local_sem.at[number]))
            loads.append(pltpu.make_async_copy(
                context.at[example, :, pl.ds(part * LANES, LANES)], held.at[tensor, example, part],
                local_sem.at[PIECES + number]))
    for copy in loads:
        copy.start()

    pl.semaphore_wait(barrier, 7)

    def chunk_copy(slot, example, part, send_sem, device):
        return pltpu.make_async_remote_copy(
            src_ref=held.at[slot, example, part], dst_ref=held.at[slot, example, part], send_sem=send_sem,
            recv_sem=ring_recv.at[slot, example, part], device_id=device, device_id_type=MESH)

    def own_copy(example, part, send_sem, device):
        return pltpu.make_async_remote_copy(
            src_ref=context.at[example, :, pl.ds(part * LANES, LANES)], dst_ref=held.at[tensor, example, part],
            send_sem=send_sem, recv_sem=ring_recv.at[tensor, example, part], device_id=device, device_id_type=MESH)

    def grad_copy(example, part):
        return pltpu.make_async_remote_copy(
            src_ref=grad.at[example, pl.ds(part * rows, rows)], dst_ref=grad_far.at[example, part],
            send_sem=grad_send.at[example, part], recv_sem=grad_recv.at[example, part],
            device_id=near, device_id_type=MESH)

    for part in range(HALVES):
        grad_copy(0, part).start()
        own_copy(0, part, far_send.at[part], far).start()
    for piece in range(PIECES):
        example, part = piece // HALVES, piece % HALVES
        own_copy(example, part, near_send.at[piece], near).start()
        if example == 1:
            own_copy(example, part, far_send.at[piece], far).start()
    for piece in range(PIECES):
        own_copy(piece // HALVES, piece % HALVES, side_send.at[piece], sibling).start()

    for turn in range(3):
        for device in around:
            pl.semaphore_signal(hello.at[turn], inc=1, device_id=device, device_id_type=MESH)
        pl.semaphore_wait(hello.at[turn], 4)

    squares[...] = jnp.zeros_like(squares)
    lanes = lax.broadcasted_iota(jnp.int32, (1, LANES), 1)
    everyone = jnp.full((1, LANES), -1, jnp.int32)
    for item in range(2 * GROUP):
        everyone = jnp.where(lanes == item, users[item], everyone)

    @pl.loop(0, 2 * GROUP)
    def _(item):
        same_user[item] = jnp.where(everyone == users[item], 1.0, 0.0)
        user_count[item] = jnp.full((1, LANES), counts[users[item]].astype(F32), F32)

    missing = lax.rem(lax.div(depth, 2) + 2, SIDE)

    def swap(main, other):
        moved = lax.rem(missing + other, SIDE)
        return jnp.where(main == missing, moved, jnp.where(main == moved, missing, main))

    def ship(tiles, tile, example, part):
        main, other = lax.div(tile, SIDE), lax.rem(tile, SIDE)
        for half in range(2):
            steps, powers = encode(tiles[2 * units * half:2 * units * (half + 1)])
            coded[tile, example, part, half, 0:units] = steps
            coded[tile, example, part, half, units] = powers
            owner = swap(main, other) if half == 0 else other

            @pl.when(owner != place[half])
            def _():
                pltpu.make_async_remote_copy(
                    src_ref=coded.at[tile, example, part, half],
                    dst_ref=early[half].at[place[half], example, (other, main)[half], part],
                    send_sem=early_send.at[half], recv_sem=early_recv.at[half],
                    device_id=(at(half, owner), tensor), device_id_type=MESH).start()

    def product(lhs, slot, example, part, tile):
        lhs = lhs.reshape((2 * rows, lhs.shape[2]))
        term = jnp.dot(lhs, held[slot, example, part], preferred_element_type=F32)
        tiles = term.reshape((4 * units, 8, LANES))
        squares[example] += jnp.sum(tiles * tiles, axis=0)
        ship(tiles, tile, example, part)

    def own_product(slot, example, part):
        product(grad_own[example], slot, example, part, slot)

    def far_product(slot, example, part):
        product(grad_far[example], slot, example, part, lax.rem(slot + 4 * away + 2 * RING, 2 * RING))

    def arrived(slot, example, part):
        chunk_copy(slot, example, part, side_send.at[0], sibling).wait_recv()

    def split(piece):
        return lax.div(piece, HALVES), lax.rem(piece, HALVES)

    for copy in loads:
        copy.wait()

    @pl.loop(0, PIECES)
    def _(piece):
        own_product(tensor, *split(piece))

    @pl.loop(0, PIECES)
    def _(piece):
        arrived(depth * 2 + 1 - core, *split(piece))
        own_product(depth * 2 + 1 - core, *split(piece))

    @pl.loop(0, PIECES)
    def _(piece):
        example, part = split(piece)
        for block, device, send_sem, side in (
                (plane(1), near, near_send.at[PIECES + piece], PIECES), (plane(-1), far, far_send.at[PIECES + piece], 2 * PIECES)):
            slot = block * 2 + core
            arrived(slot, example, part)
            chunk_copy(slot, example, part, send_sem, device).start()
            chunk_copy(slot, example, part, side_send.at[side + piece], sibling).start()
        for block in (plane(1), plane(-1)):
            own_product(block * 2 + core, example, part)
        for block in (plane(1), plane(-1)):
            arrived(block * 2 + 1 - core, example, part)
            own_product(block * 2 + 1 - core, example, part)

    for part in range(HALVES):
        grad_copy(1, part).start()
    for part in range(HALVES):
        grad_copy(0, part).wait_recv()

    @pl.loop(0, PIECES)
    def _(piece):
        example, part = split(piece)
        slot = plane(2) * 2 + core
        arrived(slot, example, part)
        chunk_copy(slot, example, part, side_send.at[3 * PIECES + piece], sibling).start()
        slot = plane(-2) * 2 + core
        arrived(slot, example, part)
        chunk_copy(slot, example, part, far_send.at[2 * PIECES + piece], far).start()
        chunk_copy(slot, example, part, side_send.at[4 * PIECES + piece], sibling).start()
        for block in (plane(2), plane(-2)):
            own_product(block * 2 + core, example, part)
        for block in (plane(2), plane(-2)):
            arrived(block * 2 + 1 - core, example, part)
            own_product(block * 2 + 1 - core, example, part)

        @pl.when(piece < HALVES)
        def _():
            for parity in range(2):
                far_product(plane(2) * 2 + parity, 0, part)

    @pl.loop(0, PIECES)
    def _(piece):
        example, part = split(piece)
        slot = plane(3) * 2 + core
        arrived(slot, example, part)
        chunk_copy(slot, example, part, side_send.at[5 * PIECES + piece], sibling).start()
        own_product(slot, example, part)
        slot = plane(3) * 2 + 1 - core
        arrived(slot, example, part)
        own_product(slot, example, part)

        @pl.when(piece < HALVES)
        def _():
            for parity in range(2):
                far_product(plane(3) * 2 + parity, 0, part)

    for part in range(HALVES):
        grad_copy(1, part).wait_recv()

    @pl.loop(0, 4)
    def _(item):
        slot = plane(2 + lax.div(item, 2)) * 2 + lax.rem(item, 2)
        lhs = grad_far[1]
        rhs = jnp.concatenate([held[slot, 1, part] for part in range(HALVES)], axis=1)
        term = jnp.dot(lhs.reshape((2 * rows, lhs.shape[2])), rhs, preferred_element_type=F32)
        tiles = term.reshape((4 * units, 8, HALVES * LANES))
        square = jnp.sum(tiles * tiles, axis=0)
        for part in range(HALVES):
            span = slice(part * LANES, (part + 1) * LANES)
            squares[1] += square[:, span]
            spare[item, part] = tiles[:, :, span]

    lanes = lax.broadcasted_iota(jnp.int32, (8, LANES), 1)

    def in_lanes(values):
        return jnp.where(lanes == 2 * data, values[0], jnp.where(lanes == 2 * data + 1, values[1], 0.0))

    own = [jnp.sum(jnp.sum(squares[example], axis=0, keepdims=True), axis=1, keepdims=True) for example in range(2)]
    square_box[tensor] = in_lanes(own)

    def square_copy(step, index):
        return pltpu.make_async_remote_copy(
            src_ref=square_box.at[tensor], dst_ref=square_box.at[tensor], send_sem=square_send.at[step],
            recv_sem=square_recv.at[index], device_id=(data, lax.rem(tensor + step, GROUP)), device_id_type=MESH)

    for step in FAR_TENSOR:
        square_copy(step, tensor).start()

    @pl.loop(0, 4)
    def _(item):
        tile = lax.rem((plane(2 + lax.div(item, 2)) + 2 * away) * 2 + lax.rem(item, 2) + 2 * RING, 2 * RING)
        for part in range(HALVES):
            ship(spare[item, part], tile, 1, part)

    @pl.loop(0, SIDE_SENDS)
    def _(index):
        chunk_copy(0, 0, 0, side_send.at[index], sibling).wait_send()

        @pl.when(index < 3 * PIECES)
        def _():
            chunk_copy(0, 0, 0, far_send.at[index], far).wait_send()

        @pl.when(index < 2 * PIECES)
        def _():
            chunk_copy(0, 0, 0, near_send.at[index], near).wait_send()

    for example in range(2):
        for part in range(HALVES):
            grad_copy(example, part).wait_send()
    for step in reversed(FAR_TENSOR):
        square_copy(step, lax.rem(tensor + step, GROUP)).wait_recv()

    norm = jnp.sqrt(jnp.sum(square_box[...], axis=0) + 1e-6)
    norm_box[data] = in_lanes((norm, norm))

    def norm_copy(step, index):
        peer = lax.rem(place[0] + step // SIDE, SIDE) * SIDE + lax.rem(place[1] + step % SIDE, SIDE)
        return pltpu.make_async_remote_copy(
            src_ref=norm_box.at[data], dst_ref=norm_box.at[data], send_sem=norm_send.at[step],
            recv_sem=norm_recv.at[peer if index is None else index], device_id=(peer, tensor), device_id_type=MESH)

    for step in FAR_DATA:
        norm_copy(step, data).start()
    for step in range(1, GROUP):
        square_copy(step, tensor).wait_send()
    for step in reversed(FAR_DATA):
        norm_copy(step, None).wait_recv()

    norms = jnp.sum(norm_box[...], axis=0)[0:1]
    user_norm = jnp.sum(same_user[...] * norms, axis=2, keepdims=True)
    count = user_count[...]
    weight[...] = jnp.minimum(1.0, clip_bound * count / user_norm) / (count * counts.shape[0])

    def all_early(dim):
        whole = early[dim].at[pl.ds(0, SIDE - 1)]
        return pltpu.make_async_remote_copy(
            src_ref=whole, dst_ref=whole, send_sem=early_send.at[dim], recv_sem=early_recv.at[dim],
            device_id=sibling, device_id_type=MESH)

    def spot(dim, turn):
        first = lax.rem((place[0] - missing if dim == 0 else missing) - place[1 - dim] * (1 - dim) - place[0] * dim + 2 * SIDE, SIDE)
        order = (first, jnp.where(first == 2, 1, 2), jnp.where((first == 1) | (first == 2), 3, 1),
                 jnp.where(first == 0, 3, 0))
        swapped = (order[0], order[2], order[1], order[3])
        step = jnp.where(core == dim, order[turn], swapped[turn])
        if dim == 0:
            other = lax.rem(place[1] + step, SIDE)
            return other, swap(place[0], other), other
        main = lax.rem(place[0] + step, SIDE)
        return main, main, place[1]

    def target(dim, turn):
        _, main, other = spot(dim, turn)
        foreign = jnp.where(main == missing, 1, 0)
        row = lax.rem(main * SIDE + other - 4 * away * foreign + GROUP, GROUP)
        return row, plane(-foreign) * 2 + core

    def late_copy(dim, turn):
        return pltpu.make_async_remote_copy(
            src_ref=late.at[dim, turn], dst_ref=final.at[dim, place[1 - dim]], send_sem=total_send.at[dim, turn],
            recv_sem=total_recv.at[dim, place[1 - dim]], device_id=target(dim, turn), device_id_type=MESH)

    def is_here(dim, turn):
        row, column = target(dim, turn)
        return (row == data) & (column == tensor)

    for dim in range(2):
        all_early(dim).wait_recv()
    for turn in range(SIDE):
        for dim in range(2):
            index, main, other = spot(dim, turn)
            both = []
            for part in range(HALVES):
                total = sum(decode(coded.at[main * SIDE + other, example, part, dim], weight[2 * data + example])
                            for example in range(2))
                for step in range(1, SIDE):
                    source = along(dim, step)
                    for example in range(2):
                        total = total + decode(early[dim].at[source, example, index, part],
                                               weight[2 * at(dim, source) + example])
                steps, powers = encode(total)
                late[dim, turn, part * units:(part + 1) * units] = steps
                both.append(powers.astype(jnp.int32))
            upper = lax.broadcasted_iota(jnp.int32, both[0].shape, 0) < 8
            late[dim, turn, 2 * units] = jnp.where(upper, both[0], both[1]).astype(jnp.int16)

            @pl.when(jnp.logical_not(is_here(dim, turn)))
            def _():
                late_copy(dim, turn).start()

            @pl.when(is_here(dim, turn))
            def _():
                pltpu.make_async_copy(
                    late.at[dim, turn], final.at[dim, place[1 - dim]], total_recv.at[dim, place[1 - dim]]).start()

    for dim in range(2):
        all_early(dim).wait_send()
    for step in range(1, GROUP):
        norm_copy(step, data).wait_send()
    for turn in range(SIDE):
        for dim in range(2):
            @pl.when(jnp.logical_not(is_here(dim, turn)))
            def _():
                late_copy(dim, turn).wait_send()

    for dim in range(2):
        for source in range(SIDE):
            pltpu.make_async_remote_copy(
                src_ref=late.at[0, 0], dst_ref=final.at[dim, source], send_sem=total_send.at[0, 0],
                recv_sem=total_recv.at[dim, source], device_id=sibling, device_id_type=MESH).wait_recv()
        for part in range(HALVES):
            total = sum(landed(final.at[dim, source], part) for source in range(SIDE))
            out[pl.ds(2 * units * dim, 2 * units), :, pl.ds(part * LANES, LANES)] = total


def per_device(context, grad, users, counts):
    examples, length, width_in = context.shape
    width_out = grad.shape[2]
    tiles = width_out // 8
    units = width_out // 32
    dma = pltpu.SemaphoreType.DMA
    vmem = pltpu.VMEM
    int16 = jnp.int16
    clip_bound = 1.5 * math.sqrt(width_in * width_out * GROUP * GROUP)
    flops = 2 * examples * length * width_in * width_out * GROUP
    result = pl.pallas_call(
        functools.partial(kernel, clip_bound),
        out_shape=vmem((tiles, 8, width_in), F32),
        in_specs=[
            pl.BlockSpec(memory_space=pl.ANY),
            pl.BlockSpec(memory_space=pl.ANY),
            pl.BlockSpec(memory_space=pltpu.SMEM),
            pl.BlockSpec(memory_space=pltpu.SMEM),
        ],
        out_specs=pl.BlockSpec(memory_space=pltpu.VMEM),
        scratch_shapes=[
            vmem((GROUP, examples, HALVES, length, LANES), context.dtype),
            vmem((examples, HALVES, 16 * units, length), grad.dtype),
            vmem((examples, HALVES, 16 * units, length), grad.dtype),
            vmem((GROUP, examples, HALVES, HALVES, units + 1, 16, LANES), int16),
            vmem((SIDE, examples, SIDE, HALVES, units + 1, 16, LANES), int16),
            vmem((SIDE, examples, SIDE, HALVES, units + 1, 16, LANES), int16),
            vmem((2, SIDE, 2 * units + 1, 16, LANES), int16),
            vmem((2, SIDE, 2 * units + 1, 16, LANES), int16),
            vmem((4, HALVES, tiles, 8, LANES), F32),
            vmem((2 * GROUP, 1, LANES), F32),
            vmem((2 * GROUP, 1, LANES), F32),
            vmem((2 * GROUP, 1, LANES), F32),
            vmem((examples, 8, LANES), F32),
            vmem((GROUP, 8, LANES), F32),
            vmem((GROUP, 8, LANES), F32),
            dma((2 * PIECES,)),
            dma((GROUP, 2, HALVES)),
            dma((3 * PIECES,)),
            dma((2 * PIECES,)),
            dma((SIDE_SENDS,)),
            dma((2, HALVES)),
            dma((2, HALVES)),
            dma((2,)),
            dma((2,)),
            dma((GROUP,)),
            dma((GROUP,)),
            dma((GROUP,)),
            dma((GROUP,)),
            dma((2, SIDE)),
            dma((2, SIDE)),
            pltpu.SemaphoreType.REGULAR((3,)),
        ],
        compiler_params=pltpu.CompilerParams(
            collective_id=0, has_side_effects=True, vmem_limit_bytes=56 * 2**20),
        cost_estimate=pl.CostEstimate(flops=flops, bytes_accessed=2 * context.size + 2 * grad.size, transcendentals=0),
    )(context, jnp.swapaxes(grad, 1, 2), users, counts)
    return result.reshape(width_out, width_in).T


def solution(mesh):
    in_specs = (P("dp", None, "tensor"), P("dp", None, "tensor"), P(), P())
    out_specs = P("dp", "tensor")
    return jax.shard_map(
        per_device, mesh=mesh, in_specs=in_specs, out_specs=out_specs, check_vma=False
    )
```

```python
import functools
import math

import jax
import jax.numpy as jnp
from jax import lax
from jax.experimental import pallas as pl
from jax.experimental.pallas import tpu as pltpu
from jax.sharding import PartitionSpec as P

MESH = pl.DeviceIdType.MESH
F32 = jnp.float32
SIDE = 4
RING = 8
GROUP = 16
LANES = 128
HALVES = 2
PIECES = 2 * HALVES
SIDE_SENDS = 6 * PIECES
STEPS = 32000.0
FAR_TENSOR = sorted(range(1, GROUP), key=lambda step: -min(step, GROUP - step))
FAR_DATA = sorted(range(1, GROUP), key=lambda step: -min(step // SIDE, SIDE - step // SIDE) - min(step % SIDE, SIDE - step % SIDE))


def encode(tiles):
    peak = jnp.max(jnp.max(jnp.abs(tiles), axis=0), axis=0, keepdims=True)
    power = jnp.ceil(jnp.log2(jnp.maximum(peak, 1e-30)))
    steps = jnp.round(tiles * (STEPS * jnp.exp2(-power))[None]).astype(jnp.int32).astype(jnp.int16)
    powers = jnp.broadcast_to(power, (16,) + power.shape[1:]).astype(jnp.int32).astype(jnp.int16)
    return steps.reshape((tiles.shape[0] // 2, 16) + tiles.shape[2:]), powers


def decode(ref, factor):
    units = ref.shape[0] - 1
    power = ref[units].astype(jnp.int32).astype(F32)[0:1]
    scale = factor * (jnp.exp2(power) * (1.0 / STEPS))
    steps = ref[0:units].astype(jnp.int32).astype(F32)
    return scale * steps.reshape((2 * units, 8) + ref.shape[2:])


def kernel(clip_bound, context, grad, users, counts, out, held, grad_own, grad_far, coded, early_x, early_y, late, final, spare,
           same_user, user_count, weight, squares, square_box, norm_box,
           local_sem, ring_recv, far_send, near_send, side_send, grad_send, grad_recv, early_send, early_recv,
           square_send, square_recv, norm_send, norm_recv, total_send, total_recv, hello):
    data, tensor = lax.axis_index("dp"), lax.axis_index("tensor")
    depth, core = lax.div(tensor, 2), lax.rem(tensor, 2)
    place = (lax.div(data, SIDE), lax.rem(data, SIDE))
    units = coded.shape[4] - 1
    early = (early_x, early_y)
    rows = 16 * units
    away = 1 - 2 * lax.rem(depth, 2)

    def plane(step):
        return lax.rem(depth + away * step + RING, RING)

    def along(dim, step):
        return lax.rem(place[dim] + step + SIDE, SIDE)

    def at(dim, value):
        return value * SIDE + place[1] if dim == 0 else place[0] * SIDE + value

    far = (data, plane(1) * 2 + core)
    near = (data, plane(-1) * 2 + core)
    sibling = (data, depth * 2 + 1 - core)
    around = tuple((at(dim, along(dim, step)), tensor) for dim in range(2) for step in (1, -1))

    barrier = pltpu.get_barrier_semaphore()
    for device in (far, near) + around + (sibling,):
        pl.semaphore_signal(barrier, inc=1, device_id=device, device_id_type=MESH)

    loads = []
    for example in range(2):
        for part in range(HALVES):
            number = example * HALVES + part
            loads.append(pltpu.make_async_copy(
                grad.at[example, pl.ds(part * rows, rows)], grad_own.at[example, part], local_sem.at[number]))
            loads.append(pltpu.make_async_copy(
                context.at[example, :, pl.ds(part * LANES, LANES)], held.at[tensor, example, part],
                local_sem.at[PIECES + number]))
    for copy in loads:
        copy.start()

    pl.semaphore_wait(barrier, 7)

    def chunk_copy(slot, example, part, send_sem, device):
        return pltpu.make_async_remote_copy(
            src_ref=held.at[slot, example, part], dst_ref=held.at[slot, example, part], send_sem=send_sem,
            recv_sem=ring_recv.at[slot, example, part], device_id=device, device_id_type=MESH)

    def own_copy(example, part, send_sem, device):
        return pltpu.make_async_remote_copy(
            src_ref=context.at[example, :, pl.ds(part * LANES, LANES)], dst_ref=held.at[tensor, example, part],
            send_sem=send_sem, recv_sem=ring_recv.at[tensor, example, part], device_id=device, device_id_type=MESH)

    def grad_copy(example, part):
        return pltpu.make_async_remote_copy(
            src_ref=grad.at[example, pl.ds(part * rows, rows)], dst_ref=grad_far.at[example, part],
            send_sem=grad_send.at[example, part], recv_sem=grad_recv.at[example, part],
            device_id=near, device_id_type=MESH)

    for part in range(HALVES):
        grad_copy(0, part).start()
        own_copy(0, part, far_send.at[part], far).start()
    for piece in range(PIECES):
        example, part = piece // HALVES, piece % HALVES
        own_copy(example, part, near_send.at[piece], near).start()
        if example == 1:
            own_copy(example, part, far_send.at[piece], far).start()
    for piece in range(PIECES):
        own_copy(piece // HALVES, piece % HALVES, side_send.at[piece], sibling).start()

    for turn in range(3):
        for device in around:
            pl.semaphore_signal(hello.at[turn], inc=1, device_id=device, device_id_type=MESH)
        pl.semaphore_wait(hello.at[turn], 4)

    squares[...] = jnp.zeros_like(squares)
    lanes = lax.broadcasted_iota(jnp.int32, (1, LANES), 1)
    everyone = jnp.full((1, LANES), -1, jnp.int32)
    for item in range(2 * GROUP):
        everyone = jnp.where(lanes == item, users[item], everyone)

    @pl.loop(0, 2 * GROUP)
    def _(item):
        same_user[item] = jnp.where(everyone == users[item], 1.0, 0.0)
        user_count[item] = jnp.full((1, LANES), counts[users[item]].astype(F32), F32)

    missing = lax.rem(lax.div(depth, 2) + 2, SIDE)

    def swap(main, other):
        moved = lax.rem(missing + other, SIDE)
        return jnp.where(main == missing, moved, jnp.where(main == moved, missing, main))

    def ship(tiles, tile, example, part):
        main, other = lax.div(tile, SIDE), lax.rem(tile, SIDE)
        for half in range(2):
            steps, powers = encode(tiles[2 * units * half:2 * units * (half + 1)])
            coded[tile, example, part, half, 0:units] = steps
            coded[tile, example, part, half, units] = powers
            owner = swap(main, other) if half == 0 else other

            @pl.when(owner != place[half])
            def _():
                pltpu.make_async_remote_copy(
                    src_ref=coded.at[tile, example, part, half],
                    dst_ref=early[half].at[place[half], example, (other, main)[half], part],
                    send_sem=early_send.at[half], recv_sem=early_recv.at[half],
                    device_id=(at(half, owner), tensor), device_id_type=MESH).start()

    def product(lhs, slot, example, part, tile):
        lhs = lhs.reshape((2 * rows, lhs.shape[2]))
        term = jnp.dot(lhs, held[slot, example, part], preferred_element_type=F32)
        tiles = term.reshape((4 * units, 8, LANES))
        squares[example] += jnp.sum(tiles * tiles, axis=0)
        ship(tiles, tile, example, part)

    def own_product(slot, example, part):
        product(grad_own[example], slot, example, part, slot)

    def far_product(slot, example, part):
        product(grad_far[example], slot, example, part, lax.rem(slot + 4 * away + 2 * RING, 2 * RING))

    def arrived(slot, example, part):
        chunk_copy(slot, example, part, side_send.at[0], sibling).wait_recv()

    def split(piece):
        return lax.div(piece, HALVES), lax.rem(piece, HALVES)

    for copy in loads:
        copy.wait()

    @pl.loop(0, PIECES)
    def _(piece):
        own_product(tensor, *split(piece))

    @pl.loop(0, PIECES)
    def _(piece):
        arrived(depth * 2 + 1 - core, *split(piece))
        own_product(depth * 2 + 1 - core, *split(piece))

    @pl.loop(0, PIECES)
    def _(piece):
        example, part = split(piece)
        for block, device, send_sem, side in (
                (plane(1), near, near_send.at[PIECES + piece], PIECES), (plane(-1), far, far_send.at[PIECES + piece], 2 * PIECES)):
            slot = block * 2 + core
            arrived(slot, example, part)
            chunk_copy(slot, example, part, send_sem, device).start()
            chunk_copy(slot, example, part, side_send.at[side + piece], sibling).start()
        for block in (plane(1), plane(-1)):
            own_product(block * 2 + core, example, part)
        for block in (plane(1), plane(-1)):
            arrived(block * 2 + 1 - core, example, part)
            own_product(block * 2 + 1 - core, example, part)

    for part in range(HALVES):
        grad_copy(1, part).start()
    for part in range(HALVES):
        grad_copy(0, part).wait_recv()

    @pl.loop(0, PIECES)
    def _(piece):
        example, part = split(piece)
        slot = plane(2) * 2 + core
        arrived(slot, example, part)
        chunk_copy(slot, example, part, side_send.at[3 * PIECES + piece], sibling).start()
        slot = plane(-2) * 2 + core
        arrived(slot, example, part)
        chunk_copy(slot, example, part, far_send.at[2 * PIECES + piece], far).start()
        chunk_copy(slot, example, part, side_send.at[4 * PIECES + piece], sibling).start()
        for block in (plane(2), plane(-2)):
            own_product(block * 2 + core, example, part)
        for block in (plane(2), plane(-2)):
            arrived(block * 2 + 1 - core, example, part)
            own_product(block * 2 + 1 - core, example, part)

        @pl.when(piece < HALVES)
        def _():
            for parity in range(2):
                far_product(plane(2) * 2 + parity, 0, part)

    @pl.loop(0, PIECES)
    def _(piece):
        example, part = split(piece)
        slot = plane(3) * 2 + core
        arrived(slot, example, part)
        chunk_copy(slot, example, part, side_send.at[5 * PIECES + piece], sibling).start()
        own_product(slot, example, part)
        slot = plane(3) * 2 + 1 - core
        arrived(slot, example, part)
        own_product(slot, example, part)

        @pl.when(piece < HALVES)
        def _():
            for parity in range(2):
                far_product(plane(3) * 2 + parity, 0, part)

    for part in range(HALVES):
        grad_copy(1, part).wait_recv()

    for item in range(4):
        slot = plane(2 + item // 2) * 2 + item % 2
        lhs = grad_far[1]
        rhs = jnp.concatenate([held[slot, 1, part] for part in range(HALVES)], axis=1)
        term = jnp.dot(lhs.reshape((2 * rows, lhs.shape[2])), rhs, preferred_element_type=F32)
        tiles = term.reshape((4 * units, 8, HALVES * LANES))
        square = jnp.sum(tiles * tiles, axis=0)
        for part in range(HALVES):
            span = slice(part * LANES, (part + 1) * LANES)
            squares[1] += square[:, span]
            spare[item, part] = tiles[:, :, span]

    lanes = lax.broadcasted_iota(jnp.int32, (8, LANES), 1)

    def in_lanes(values):
        return jnp.where(lanes == 2 * data, values[0], jnp.where(lanes == 2 * data + 1, values[1], 0.0))

    own = [jnp.sum(jnp.sum(squares[example], axis=0, keepdims=True), axis=1, keepdims=True) for example in range(2)]
    square_box[tensor] = in_lanes(own)

    def square_copy(step, index):
        return pltpu.make_async_remote_copy(
            src_ref=square_box.at[tensor], dst_ref=square_box.at[tensor], send_sem=square_send.at[step],
            recv_sem=square_recv.at[index], device_id=(data, lax.rem(tensor + step, GROUP)), device_id_type=MESH)

    for step in FAR_TENSOR:
        square_copy(step, tensor).start()

    @pl.loop(0, 4)
    def _(item):
        tile = lax.rem((plane(2 + lax.div(item, 2)) + 2 * away) * 2 + lax.rem(item, 2) + 2 * RING, 2 * RING)
        for part in range(HALVES):
            ship(spare[item, part], tile, 1, part)

    @pl.loop(0, SIDE_SENDS)
    def _(index):
        chunk_copy(0, 0, 0, side_send.at[index], sibling).wait_send()

        @pl.when(index < 3 * PIECES)
        def _():
            chunk_copy(0, 0, 0, far_send.at[index], far).wait_send()

        @pl.when(index < 2 * PIECES)
        def _():
            chunk_copy(0, 0, 0, near_send.at[index], near).wait_send()

    for example in range(2):
        for part in range(HALVES):
            grad_copy(example, part).wait_send()
    for step in reversed(FAR_TENSOR):
        square_copy(step, lax.rem(tensor + step, GROUP)).wait_recv()

    norm = jnp.sqrt(jnp.sum(square_box[...], axis=0) + 1e-6)
    norm_box[data] = in_lanes((norm, norm))

    def norm_copy(step, index):
        peer = lax.rem(place[0] + step // SIDE, SIDE) * SIDE + lax.rem(place[1] + step % SIDE, SIDE)
        return pltpu.make_async_remote_copy(
            src_ref=norm_box.at[data], dst_ref=norm_box.at[data], send_sem=norm_send.at[step],
            recv_sem=norm_recv.at[peer if index is None else index], device_id=(peer, tensor), device_id_type=MESH)

    for step in FAR_DATA:
        norm_copy(step, data).start()
    for step in range(1, GROUP):
        square_copy(step, tensor).wait_send()
    for step in reversed(FAR_DATA):
        norm_copy(step, None).wait_recv()

    norms = jnp.sum(norm_box[...], axis=0)[0:1]
    user_norm = jnp.sum(same_user[...] * norms, axis=2, keepdims=True)
    count = user_count[...]
    weight[...] = jnp.minimum(1.0, clip_bound * count / user_norm) / (count * counts.shape[0])

    def all_early(dim):
        whole = early[dim].at[pl.ds(0, SIDE - 1)]
        return pltpu.make_async_remote_copy(
            src_ref=whole, dst_ref=whole, send_sem=early_send.at[dim], recv_sem=early_recv.at[dim],
            device_id=sibling, device_id_type=MESH)

    def spot(dim, turn):
        first = lax.rem((place[0] - missing if dim == 0 else missing) - place[1 - dim] * (1 - dim) - place[0] * dim + 2 * SIDE, SIDE)
        order = (first, jnp.where(first == 2, 1, 2), jnp.where((first == 1) | (first == 2), 3, 1),
                 jnp.where(first == 0, 3, 0))
        swapped = (order[0], order[2], order[1], order[3])
        step = jnp.where(core == dim, order[turn], swapped[turn])
        if dim == 0:
            other = lax.rem(place[1] + step, SIDE)
            return other, swap(place[0], other), other
        main = lax.rem(place[0] + step, SIDE)
        return main, main, place[1]

    def target(dim, turn):
        _, main, other = spot(dim, turn)
        foreign = jnp.where(main == missing, 1, 0)
        row = lax.rem(main * SIDE + other - 4 * away * foreign + GROUP, GROUP)
        return row, plane(-foreign) * 2 + core

    def late_copy(dim, turn):
        return pltpu.make_async_remote_copy(
            src_ref=late.at[dim, turn], dst_ref=final.at[dim, place[1 - dim]], send_sem=total_send.at[dim, turn],
            recv_sem=total_recv.at[dim, place[1 - dim]], device_id=target(dim, turn), device_id_type=MESH)

    def is_here(dim, turn):
        row, column = target(dim, turn)
        return (row == data) & (column == tensor)

    for dim in range(2):
        all_early(dim).wait_recv()
    for turn in range(SIDE):
        for dim in range(2):
            index, main, other = spot(dim, turn)
            for part in range(HALVES):
                total = sum(decode(coded.at[main * SIDE + other, example, part, dim], weight[2 * data + example])
                            for example in range(2))
                for step in range(1, SIDE):
                    source = along(dim, step)
                    for example in range(2):
                        total = total + decode(early[dim].at[source, example, index, part],
                                               weight[2 * at(dim, source) + example])
                steps, powers = encode(total)
                late[dim, turn, part, 0:units] = steps
                late[dim, turn, part, units] = powers

            @pl.when(jnp.logical_not(is_here(dim, turn)))
            def _():
                late_copy(dim, turn).start()

            @pl.when(is_here(dim, turn))
            def _():
                pltpu.make_async_copy(
                    late.at[dim, turn], final.at[dim, place[1 - dim]], total_recv.at[dim, place[1 - dim]]).start()

    for dim in range(2):
        all_early(dim).wait_send()
    for step in range(1, GROUP):
        norm_copy(step, data).wait_send()
    for turn in range(SIDE):
        for dim in range(2):
            @pl.when(jnp.logical_not(is_here(dim, turn)))
            def _():
                late_copy(dim, turn).wait_send()

    for dim in range(2):
        for source in range(SIDE):
            pltpu.make_async_remote_copy(
                src_ref=late.at[0, 0], dst_ref=final.at[dim, source], send_sem=total_send.at[0, 0],
                recv_sem=total_recv.at[dim, source], device_id=sibling, device_id_type=MESH).wait_recv()
        for part in range(HALVES):
            total = sum(decode(final.at[dim, source, part], 1.0) for source in range(SIDE))
            out[pl.ds(2 * units * dim, 2 * units), :, pl.ds(part * LANES, LANES)] = total


def per_device(context, grad, users, counts):
    examples, length, width_in = context.shape
    width_out = grad.shape[2]
    tiles = width_out // 8
    units = width_out // 32
    dma = pltpu.SemaphoreType.DMA
    vmem = pltpu.VMEM
    int16 = jnp.int16
    clip_bound = 1.5 * math.sqrt(width_in * width_out * GROUP * GROUP)
    flops = 2 * examples * length * width_in * width_out * GROUP
    result = pl.pallas_call(
        functools.partial(kernel, clip_bound),
        out_shape=vmem((tiles, 8, width_in), F32),
        in_specs=[
            pl.BlockSpec(memory_space=pl.ANY),
            pl.BlockSpec(memory_space=pl.ANY),
            pl.BlockSpec(memory_space=pltpu.SMEM),
            pl.BlockSpec(memory_space=pltpu.SMEM),
        ],
        out_specs=pl.BlockSpec(memory_space=pltpu.VMEM),
        scratch_shapes=[
            vmem((GROUP, examples, HALVES, length, LANES), context.dtype),
            vmem((examples, HALVES, 16 * units, length), grad.dtype),
            vmem((examples, HALVES, 16 * units, length), grad.dtype),
            vmem((GROUP, examples, HALVES, HALVES, units + 1, 16, LANES), int16),
            vmem((SIDE, examples, SIDE, HALVES, units + 1, 16, LANES), int16),
            vmem((SIDE, examples, SIDE, HALVES, units + 1, 16, LANES), int16),
            vmem((2, SIDE, HALVES, units + 1, 16, LANES), int16),
            vmem((2, SIDE, HALVES, units + 1, 16, LANES), int16),
            vmem((4, HALVES, tiles, 8, LANES), F32),
            vmem((2 * GROUP, 1, LANES), F32),
            vmem((2 * GROUP, 1, LANES), F32),
            vmem((2 * GROUP, 1, LANES), F32),
            vmem((examples, 8, LANES), F32),
            vmem((GROUP, 8, LANES), F32),
            vmem((GROUP, 8, LANES), F32),
            dma((2 * PIECES,)),
            dma((GROUP, 2, HALVES)),
            dma((3 * PIECES,)),
            dma((2 * PIECES,)),
            dma((SIDE_SENDS,)),
            dma((2, HALVES)),
            dma((2, HALVES)),
            dma((2,)),
            dma((2,)),
            dma((GROUP,)),
            dma((GROUP,)),
            dma((GROUP,)),
            dma((GROUP,)),
            dma((2, SIDE)),
            dma((2, SIDE)),
            pltpu.SemaphoreType.REGULAR((3,)),
        ],
        compiler_params=pltpu.CompilerParams(
            collective_id=0, has_side_effects=True, vmem_limit_bytes=56 * 2**20),
        cost_estimate=pl.CostEstimate(flops=flops, bytes_accessed=2 * context.size + 2 * grad.size, transcendentals=0),
    )(context, jnp.swapaxes(grad, 1, 2), users, counts)
    return result.reshape(width_out, width_in).T


def solution(mesh):
    in_specs = (P("dp", None, "tensor"), P("dp", None, "tensor"), P(), P())
    out_specs = P("dp", "tensor")
    return jax.shard_map(
        per_device, mesh=mesh, in_specs=in_specs, out_specs=out_specs, check_vma=False
    )
```
